256 devices in a mesh: blk: 16 (over z_lo, y), grain: 16 (over z_hi, x, core).
Axes of the slice: x: 4, y: 4, z: 8 (z_hi: 2, z_lo: 4; z = z_hi * 4 + z_lo), core: 2. Of those that a mesh axis runs over, the one named last changes fastest.
Arguments:
- order: float32 [256, 512, 2048], P('grain', 'blk'), may hold values from -0.6 to 0.6
- grain_ids: int32 [256], P('grain'), may hold values from 0 to 255, each once
- counts: int32 [16], P('grain'), may hold values from 1 to 16, as said below
- labels: int32 [512, 2048], P('blk'), may hold values from 0 to 255
Outputs:
- evolved: float32 [256, 512, 2048], P('grain', 'blk')
The draws below stay inside these ranges and needn't reach their ends.
Inputs may be any that keep to these rules, and one draw needn't show every extreme that they name: `counts`: each grain group has 1 to 16 active slots, some group exactly 16.
All inputs are finite; a program needn't handle non-finite values.
Results may differ from the reference program's by a relative error of at most 0.0003.
Values sent between devices are 32-bit elements; how exact they have to be, the bound alone decides.
A program may use at most 128 MiB of HBM per device.

```python
import jax
import jax.numpy as jnp
from jax import lax

P_SIZE = 256
NY = 64
NZ = 32
P_DEV = 16
NX = 512
N_GRAIN = 16


def draw_counts(key, part):
    key = jax.random.fold_in(key, 7)
    first, second = jax.random.split(key)
    values = jax.random.randint(first, (N_GRAIN,), 1, 3 * P_DEV // 4 + 1)
    where_full = jax.random.randint(second, (), 0, N_GRAIN)
    return values.at[where_full].set(P_DEV).astype(jnp.int32)


def periodic_gap(first, second, length):
    apart = jnp.abs(first - second)
    return jnp.minimum(apart, length - apart)


def draw_labels(key, part):
    key = jax.random.fold_in(key, 11)
    seeds = max(NX // 16, 4)
    key_x, key_y, key_z, key_lab = jax.random.split(key, 4)
    seed_x = jax.random.randint(key_x, (seeds,), 0, NX)
    seed_y = jax.random.randint(key_y, (seeds,), 0, NY)
    seed_z = jax.random.randint(key_z, (seeds,), 0, NZ)
    seed_lab = jax.random.randint(key_lab, (seeds,), 0, P_SIZE)
    seed_lab = seed_lab.at[0].set(P_SIZE - 1).at[1].set(0)
    cell = jnp.arange(NY * NZ, dtype=jnp.int32)
    cell_y = cell // NZ
    cell_z = cell % NZ
    seed_index = jnp.arange(seeds, dtype=jnp.int32)

    def plane(xpos):
        gap_x = periodic_gap(xpos, seed_x, NX)
        gap_y = periodic_gap(cell_y[:, None], seed_y[None, :], NY)
        gap_z = periodic_gap(cell_z[:, None], seed_z[None, :], NZ)
        dist = gap_x[None, :] ** 2 + gap_y ** 2 + gap_z ** 2
        score = dist * seeds + seed_index[None, :]
        nearest = jnp.min(score, axis=1) % seeds
        return seed_lab[nearest]
    return lax.map(plane, jnp.arange(NX, dtype=jnp.int32)).astype(jnp.int32)


def block_levels(stream_key, dims, shards, smallest, high):
    factor_of = 1.0
    for position, shards_of in shards:
        draws = jax.random.uniform(jax.random.fold_in(jax.random.fold_in(stream_key, 6), position), (shards_of,), jnp.float32, smallest / len(shards), high / len(shards))
        factor_of = factor_of * jnp.repeat(jnp.exp(draws), dims[position] // shards_of).reshape((-1,) + (1,) * (len(dims) - 1 - position))
    return factor_of


def gaussian(stream_key, extent, width, bound, pieces=(), held_as=jnp.bfloat16):
    gain = block_levels(stream_key, extent, pieces, -0.22, 0.18) if pieces else 1.0
    array = jax.random.normal(stream_key, extent, jnp.float32) * width * gain
    return jnp.minimum(jnp.maximum(array, -bound), bound).astype(held_as)


def setup_inputs(seed: int = 0) -> dict:
    key_list = jax.random.split(jax.random.key(seed), 5)
    return {
        "order": gaussian(key_list[0], (P_SIZE, NX, NY * NZ), 0.15, 0.6, ((0, 16), (1, 16)), jnp.float32),
        "grain_ids": jax.random.permutation(key_list[1], P_SIZE).astype(jnp.int32),
        "counts": draw_counts(jax.random.fold_in(key_list[4], 71), 0),
        "labels": draw_labels(jax.random.fold_in(key_list[4], 71), 0),
    }


def laplace(field):
    count = field.shape[0]
    cube = field.reshape(count, NX, NY, NZ)
    total = jnp.roll(cube, 1, 1) + jnp.roll(cube, -1, 1)
    total = total + jnp.roll(cube, 1, 2) + jnp.roll(cube, -1, 2)
    total = total + jnp.roll(cube, 1, 3) + jnp.roll(cube, -1, 3)
    return (total - 6.0 * cube).reshape(count, NX, NY * NZ)


def reference(order, grain_ids, counts, labels):
    slot_pos = jnp.arange(P_SIZE, dtype=jnp.int32) % P_DEV
    group_of = jnp.arange(P_SIZE, dtype=jnp.int32) // P_DEV
    act = (slot_pos < counts[group_of]).astype(jnp.float32)
    groups = P_SIZE // P_DEV
    act_blocks = act.reshape(groups, P_DEV)
    id_blocks = grain_ids.reshape(groups, P_DEV)
    eta = (order * act[:, None, None]).reshape(groups, P_DEV, NX, NY * NZ)
    for step in range(2):
        coupling = jnp.sum(lax.map(lambda b: jnp.sum(b * b, axis=0), eta), axis=0)

        def update(items):
            block, act_row, id_row = items
            mark = (labels[None, :, :] == id_row[:, None, None]).astype(jnp.float32)
            force = -block + block ** 3 + 3.0 * block * (coupling[None] - block * block) - 2.0 * laplace(block) - 2.0 * mark
            return act_row[:, None, None] * (block - 0.075 * force)

        eta = lax.map(update, (eta, act_blocks, id_blocks))
    return eta.reshape(P_SIZE, NX, NY * NZ)
```

```python
import functools

import jax
import jax.numpy as jnp
from jax import lax
from jax.experimental import pallas as pl
from jax.experimental.pallas import tpu as pltpu
from jax.sharding import PartitionSpec as P

NZ = 32
LANES = 128
SUB = 8
SLOTS = 16
ROWS = 32
BLKS = 16
HALF = BLKS // 2
CHUNK = 2
NX4 = 4
TILES = ROWS // SUB
STRIDE = BLKS * ROWS
MESH = pl.DeviceIdType.MESH
F32 = jnp.float32


def plane_sum(ref, seg, left, right, row, lane, zpos):
    base = row + seg * ROWS
    out = []
    for r in range(TILES):
        at = base + SUB * r
        c = ref[pl.ds(pl.multiple_of(at, SUB), SUB), :]
        nxt = ref[pl.ds(pl.multiple_of(row + right * ROWS + SUB * r, SUB), SUB), :]
        prv = ref[pl.ds(pl.multiple_of(row + left * ROWS + SUB * r, SUB), SUB), :]
        up_x = ref[pl.ds(at + 1, SUB), :]
        dn_x = ref[pl.ds(at - 1, SUB), :]
        sub = lax.broadcasted_iota(jnp.int32, (SUB, LANES), 0)
        if r == TILES - 1:
            up_x = jnp.where(sub == SUB - 1, 0.0, up_x)
        if r == 0:
            dn_x = jnp.where(sub == 0, 0.0, dn_x)
        up_y = pltpu.roll(jnp.where(lane < NZ, nxt, c), LANES - NZ, 1)
        dn_y = pltpu.roll(jnp.where(lane >= LANES - NZ, prv, c), NZ, 1)
        up_z = jnp.where(zpos == NZ - 1, pltpu.roll(c, NZ - 1, 1), pltpu.roll(c, LANES - 1, 1))
        dn_z = jnp.where(zpos == 0, pltpu.roll(c, LANES - NZ + 1, 1), pltpu.roll(c, 1, 1))
        out.append((c, (up_x + dn_x) + (up_y + dn_y) + (up_z + dn_z)))
    return out


def kernel(order, ids, counts, labels, e1, u2, s2, e0, lab, p, r1, r2, r3, t, s1,
           hs, hr, load_sem, lab_sem, send_sem, recv_sem, hsend, hrecv):
    b = lax.axis_index("blk")
    g = lax.axis_index("grain")
    nb = lax.axis_size("blk")
    core = lax.rem(g, 2)
    xi = lax.rem(lax.div(g, 2), NX4)
    zh = lax.div(g, 2 * NX4)

    def grain(z, x, c):
        return (z * NX4 + x) * 2 + c

    sibling = (b, grain(zh, xi, 1 - core))
    zpeer = (b, grain(1 - zh, xi, core))
    xpeer = {d: (b, grain(zh, lax.rem(xi + d, NX4), core)) for d in (1, 2, 3)}
    after = (lax.rem(b + 1, nb), g)
    before = (lax.rem(b + nb - 1, nb), g)
    partners = [sibling, zpeer, xpeer[1], xpeer[2], xpeer[3], after, before]

    def load(j):
        cols = pl.ds(pl.multiple_of(j * LANES, LANES), LANES)
        return pltpu.make_async_copy(order.at[:, :, cols], e0.at[pl.ds(1, SLOTS), j], load_sem.at[j])

    first = HALF * (1 - core)

    def start_load(k, carry):
        load(lax.rem(first + k, BLKS)).start()
        return carry

    lax.fori_loop(0, BLKS, start_load, 0)
    lab_copy = pltpu.make_async_copy(labels, lab, lab_sem)
    lab_copy.start()

    barrier = pltpu.get_barrier_semaphore()
    for who in partners:
        pl.semaphore_signal(barrier, inc=1, device_id=who, device_id_type=MESH)

    count = counts[0]
    act = [jnp.where(s < count, 1.0, 0.0).astype(F32) for s in range(SLOTS)]

    e0f = e0.reshape((SLOTS + 2) * BLKS * ROWS, LANES)
    e1f = e1.reshape((SLOTS + 2) * BLKS * ROWS, LANES)
    u2f = u2.reshape(SLOTS * BLKS * ROWS, LANES)

    def edges(flat, step, j):
        for side, row in ((0, 0), (1, ROWS - 1)):
            for half in range(2):
                start = (SUB * half + 1) * STRIDE + j * ROWS + row
                hs[step, side, j, pl.ds(SUB * half, SUB), :] = flat[pl.ds(start, SUB, stride=STRIDE), :]

    def add_halo(flat, offset, step):
        def one(j, carry):
            for side, row in ((0, 0), (1, ROWS - 1)):
                for half in range(2):
                    start = (SUB * half + offset) * STRIDE + j * ROWS + row
                    where = pl.ds(start, SUB, stride=STRIDE)
                    flat[where, :] = flat[where, :] + actcol[half] * hr[step, side, j, pl.ds(SUB * half, SUB), :]
            return carry
        lax.fori_loop(0, BLKS, one, 0)

    sub8 = lax.broadcasted_iota(jnp.int32, (SUB, LANES), 0)
    actcol = [jnp.where(sub8 + SUB * half < count, 0.15, 0.0).astype(F32) for half in range(2)]


    def core_send(rnd, h):
        return pltpu.make_async_remote_copy(
            p.at[rnd, pl.ds(HALF * (1 - h), HALF)], r1.at[rnd],
            send_sem.at[rnd, 0], recv_sem.at[rnd, 0], device_id=sibling, device_id_type=MESH)

    def chunk_at(h, x):
        return pl.ds(HALF * h + CHUNK * x, CHUNK)

    def x_send(rnd, h, d):
        return pltpu.make_async_remote_copy(
            p.at[rnd, chunk_at(h, lax.rem(xi + d, NX4))], r2.at[rnd, d - 1],
            send_sem.at[rnd, d], recv_sem.at[rnd, d], device_id=xpeer[d], device_id_type=MESH)

    def z_send(rnd):
        return pltpu.make_async_remote_copy(
            t.at[rnd], r3.at[rnd],
            send_sem.at[rnd, 4], recv_sem.at[rnd, 4], device_id=zpeer, device_id_type=MESH)

    def ag_send(rnd, h, total, d):
        own = total.at[chunk_at(h, xi)]
        return pltpu.make_async_remote_copy(
            own, own, send_sem.at[rnd, 4 + d], recv_sem.at[rnd, 4 + d],
            device_id=xpeer[d], device_id_type=MESH)

    def ag_recv(rnd, h, total, d):
        got = total.at[chunk_at(h, lax.rem(xi + NX4 - d, NX4))]
        return pltpu.make_async_remote_copy(
            got, got, send_sem.at[rnd, 4 + d], recv_sem.at[rnd, 4 + d],
            device_id=xpeer[d], device_id_type=MESH)

    def fwd(rnd, h, total, d):
        got = total.at[chunk_at(h, lax.rem(xi + NX4 - d, NX4))]
        return pltpu.make_async_remote_copy(
            got, got, send_sem.at[rnd, 8 + d], recv_sem.at[rnd, 8 + d],
            device_id=sibling, device_id_type=MESH)

    def halo(step, side):
        return pltpu.make_async_remote_copy(
            hs.at[step, side], hr.at[step, 1 - side],
            hsend.at[step, side], hrecv.at[step, 1 - side],
            device_id=before if side == 0 else after, device_id_type=MESH)

    def reduce_chunk(rnd, h, x):
        for i in range(CHUNK):
            k = CHUNK * x + i
            p[rnd, HALF * h + k] = p[rnd, HALF * h + k] + r1[rnd, k]

    def pass1(k, carry):
        j = lax.rem(first + k, BLKS)
        load(j).wait()
        acc = [jnp.zeros((SUB, LANES), F32) for _ in range(TILES)]
        for s in range(SLOTS):
            for r in range(TILES):
                c = e0[s + 1, j, pl.ds(SUB * r, SUB), :]
                acc[r] = acc[r] + (c * act[s]) * c
        for r in range(TILES):
            p[0, j, pl.ds(SUB * r, SUB), :] = acc[r]
        edges(e0f, 0, j)
        return carry

    lane = lax.broadcasted_iota(jnp.int32, (SUB, LANES), 1)
    zpos = lax.rem(lane, NZ)

    def linear(src, dst, dst_shift, s_lo, s_hi, masked):
        def one(i, carry):
            s = s_lo + lax.div(i, BLKS // 4)
            jb = lax.rem(i, BLKS // 4) * 4
            on = jnp.where(s < count, 1.0, 0.0).astype(F32)
            gid = jnp.where(s < count, ids[s], -1)
            row = (s + 1) * STRIDE
            for jj in range(4):
                j = jb + jj
                left = lax.rem(j + BLKS - 1, BLKS)
                right = lax.rem(j + 1, BLKS)
                for r, (c, nb_sum) in enumerate(plane_sum(src, j, left, right, row, lane, zpos)):
                    labs = lab[pl.ds(SUB * r, SUB), pl.ds(pl.multiple_of(j * LANES, LANES), LANES)]
                    mark = jnp.where(labs == gid, 0.15, 0.0).astype(F32)
                    val = 0.15 * nb_sum + c * (0.175 + 0.15 * (c * c))
                    if not masked:
                        val = val * on
                    val = val + mark
                    at = row + j * ROWS + SUB * r + dst_shift
                    dst[pl.ds(pl.multiple_of(at, SUB), SUB), :] = val
            return carry
        lax.fori_loop(0, (s_hi - s_lo) * (BLKS // 4), one, 0)

    def pass2(k, carry):
        j = k
        tot = [0.225 * s1[j, pl.ds(SUB * r, SUB), :] for r in range(TILES)]
        acc = [jnp.zeros((SUB, LANES), F32) for _ in range(TILES)]
        for s in range(SLOTS):
            for r in range(TILES):
                rows = pl.ds(SUB * r, SUB)
                v = e1[s + 1, j, rows, :] - (e0[s + 1, j, rows, :] * act[s]) * tot[r]
                e1[s + 1, j, rows, :] = v
                acc[r] = acc[r] + v * v
        for r in range(TILES):
            p[1, j, pl.ds(SUB * r, SUB), :] = acc[r]
        edges(e1f, 1, j)
        return carry

    def exchange(rnd, h, total, seg, halo_step):
        core_send(rnd, h).wait_recv()
        for d in (2, 1, 3):
            reduce_chunk(rnd, h, lax.rem(xi + d, NX4))
            x_send(rnd, h, d).start()
        halo(halo_step, 0).start()
        halo(halo_step, 1).start()
        reduce_chunk(rnd, h, xi)
        seg(0)
        for d in (1, 3, 2):
            x_send(rnd, h, d).wait_recv()
        for i in range(CHUNK):
            mine = p[rnd, HALF * h + CHUNK * xi + i]
            t[rnd, i] = (mine + r2[rnd, 1, i]) + (r2[rnd, 0, i] + r2[rnd, 2, i])
        z_send(rnd).start()
        seg(1)
        z_send(rnd).wait_recv()
        for i in range(CHUNK):
            total[HALF * h + CHUNK * xi + i] = t[rnd, i] + r3[rnd, i]
        for d in (2, 1, 3):
            ag_send(rnd, h, total, d).start()
        fwd(rnd, h, total, 0).start()
        seg(2)
        for d in (1, 3, 2):
            ag_recv(rnd, h, total, d).wait_recv()
            fwd(rnd, h, total, d).start()

    def finish(rnd, h, total):
        for d in range(4):
            other = total.at[chunk_at(1 - h, lax.rem(xi + NX4 - d, NX4))]
            pltpu.make_async_remote_copy(
                other, other, send_sem.at[rnd, 8 + d], recv_sem.at[rnd, 8 + d],
                device_id=sibling, device_id_type=MESH).wait_recv()

    cuts = (0, 5, 10, 16)

    lax.fori_loop(0, HALF, pass1, 0)
    pl.semaphore_wait(barrier, len(partners))
    core_send(0, core).start()
    lax.fori_loop(HALF, BLKS, pass1, 0)
    lab_copy.wait()
    exchange(0, core, s1, lambda k: linear(e0f, e1f, 0, cuts[k], cuts[k + 1], False), 0)
    halo(0, 0).wait_recv()
    halo(0, 1).wait_recv()
    add_halo(e1f, 1, 0)
    lax.fori_loop(HALF * core, HALF * core + HALF, pass2, 0)
    core_send(1, 1 - core).start()
    finish(0, core, s1)
    lax.fori_loop(HALF * (1 - core), HALF * (1 - core) + HALF, pass2, 0)
    exchange(1, 1 - core, s2, lambda k: linear(e1f, u2f, -STRIDE, cuts[k], cuts[k + 1], True), 1)
    halo(1, 0).wait_recv()
    halo(1, 1).wait_recv()
    add_halo(u2f, 0, 1)
    finish(1, 1 - core, s2)

    for rnd, h, total in ((0, core, s1), (1, 1 - core, s2)):
        core_send(rnd, h).wait_send()
        for d in (1, 2, 3):
            x_send(rnd, h, d).wait_send()
            ag_send(rnd, h, total, d).wait_send()
        z_send(rnd).wait_send()
        for d in range(4):
            fwd(rnd, h, total, d).wait_send()
        for side in range(2):
            halo(rnd, side).wait_send()


def last(e1, u2, s2, out, stage, sem):
    def copy(s):
        return pltpu.make_async_copy(stage.at[s], out.at[s], sem.at[s])

    def one(s, carry):
        def blocks(j, carry):
            cols = pl.ds(pl.multiple_of(j * LANES, LANES), LANES)
            for r in range(TILES):
                rows = pl.ds(SUB * r, SUB)
                stage[s, rows, cols] = u2[s, j, rows, :] - e1[s + 1, j, rows, :] * (0.225 * s2[j, rows, :])
            return carry
        lax.fori_loop(0, BLKS, blocks, 0, unroll=4)
        copy(s).start()
        return carry

    lax.fori_loop(0, SLOTS, one, 0)

    def drain(s, carry):
        copy(s).wait()
        return carry
    lax.fori_loop(0, SLOTS, drain, 0)


def body(order, grain_ids, counts, labels):
    any_space = pl.BlockSpec(memory_space=pltpu.HBM)
    smem = pl.BlockSpec(memory_space=pltpu.SMEM)
    vmem = pl.BlockSpec(memory_space=pltpu.VMEM)
    order = pltpu.with_memory_space_constraint(order, pltpu.HBM)
    labels = pltpu.with_memory_space_constraint(labels, pltpu.HBM)
    e1, u2, s2 = pl.pallas_call(
        kernel,
        out_shape=(
            pltpu.VMEM((SLOTS + 2, BLKS, ROWS, LANES), F32),
            pltpu.VMEM((SLOTS, BLKS, ROWS, LANES), F32),
            pltpu.VMEM((BLKS, ROWS, LANES), F32),
        ),
        in_specs=[any_space, smem, smem, any_space],
        out_specs=(vmem, vmem, vmem),
        scratch_shapes=[
            pltpu.VMEM((SLOTS + 2, BLKS, ROWS, LANES), F32),
            pltpu.VMEM((ROWS, BLKS * LANES), jnp.int32),
            pltpu.VMEM((2, BLKS, ROWS, LANES), F32),
            pltpu.VMEM((2, HALF, ROWS, LANES), F32),
            pltpu.VMEM((2, 3, CHUNK, ROWS, LANES), F32),
            pltpu.VMEM((2, CHUNK, ROWS, LANES), F32),
            pltpu.VMEM((2, CHUNK, ROWS, LANES), F32),
            pltpu.VMEM((BLKS, ROWS, LANES), F32),
            pltpu.VMEM((2, 2, BLKS, SLOTS, LANES), F32),
            pltpu.VMEM((2, 2, BLKS, SLOTS, LANES), F32),
            pltpu.SemaphoreType.DMA((BLKS,)),
            pltpu.SemaphoreType.DMA,
            pltpu.SemaphoreType.DMA((2, 12)),
            pltpu.SemaphoreType.DMA((2, 12)),
            pltpu.SemaphoreType.DMA((2, 2)),
            pltpu.SemaphoreType.DMA((2, 2)),
        ],
        compiler_params=pltpu.CompilerParams(
            collective_id=0, has_side_effects=True, vmem_limit_bytes=32 * 1024 * 1024),
        name="steps",
    )(order, grain_ids, counts, labels)
    return pl.pallas_call(
        last,
        out_shape=jax.ShapeDtypeStruct(order.shape, F32),
        in_specs=[vmem, vmem, vmem],
        out_specs=any_space,
        scratch_shapes=[
            pltpu.VMEM((SLOTS, ROWS, BLKS * LANES), F32),
            pltpu.SemaphoreType.DMA((SLOTS,)),
        ],
        compiler_params=pltpu.CompilerParams(vmem_limit_bytes=32 * 1024 * 1024),
        name="last",
    )(e1, u2, s2)


def solution(mesh):
    placed = (P("grain", "blk", None), P("grain"), P("grain"), P("blk", None))
    return jax.shard_map(
        body, mesh=mesh, in_specs=placed, out_specs=P("grain", "blk", None), check_vma=False
    )
```

```python
import functools

import jax
import jax.numpy as jnp
from jax import lax
from jax.experimental import pallas as pl
from jax.experimental.pallas import tpu as pltpu
from jax.sharding import PartitionSpec as P

NZ = 32
LANES = 128
SUB = 8
SLOTS = 16
ROWS = 32
BLKS = 16
HALF = BLKS // 2
CHUNK = 2
NX4 = 4
TILES = ROWS // SUB
STRIDE = BLKS * ROWS
MESH = pl.DeviceIdType.MESH
F32 = jnp.float32


def stencil_weights(w):
    k = lax.rem(lax.broadcasted_iota(jnp.int32, (2 * LANES, 2 * LANES), 0), LANES)
    n = lax.broadcasted_iota(jnp.int32, (2 * LANES, 2 * LANES), 1)
    m = lax.rem(n, LANES)
    same_y = lax.div(k, NZ) == lax.div(m, NZ)
    dz = lax.rem(m - k + LANES, NZ)
    z_side = same_y & ((dz == 1) | (dz == NZ - 1))
    y_side = (m - k == NZ) | (k - m == NZ)
    wrap = (m - k == LANES - NZ) | (k - m == LANES - NZ)
    inside = jnp.where(z_side, 1.0, 0.0) + jnp.where(y_side, 1.0, 0.0)
    w[...] = jnp.where(n < LANES, inside, jnp.where(wrap, 1.0, 0.0)).astype(jnp.bfloat16)


def split(c):
    hi = c.astype(jnp.bfloat16)
    lo = (c - hi.astype(F32)).astype(jnp.bfloat16)
    return hi, lo


def kernel(order, ids_hbm, counts, labels, e1, u2, s2, ids, w, x, ya, yb, e0, lab, p, r1, r2, r3, t, s1,
           hs, hr, load_sem, lab_sem, small_sem, send_sem, recv_sem, hsend, hrecv):
    b = lax.axis_index("blk")
    g = lax.axis_index("grain")
    nb = lax.axis_size("blk")
    core = lax.rem(g, 2)
    xi = lax.rem(lax.div(g, 2), NX4)
    zh = lax.div(g, 2 * NX4)

    def grain(z, x, c):
        return (z * NX4 + x) * 2 + c

    sibling = (b, grain(zh, xi, 1 - core))
    zpeer = (b, grain(1 - zh, xi, core))
    xpeer = {d: (b, grain(zh, lax.rem(xi + d, NX4), core)) for d in (1, 2, 3)}
    after = (lax.rem(b + 1, nb), g)
    before = (lax.rem(b + nb - 1, nb), g)
    partners = [sibling, zpeer, xpeer[1], xpeer[2], xpeer[3], after, before]

    def load(j):
        cols = pl.ds(pl.multiple_of(j * LANES, LANES), LANES)
        return pltpu.make_async_copy(order.at[:, :, cols], e0.at[pl.ds(1, SLOTS), j], load_sem.at[j])

    first = HALF * (1 - core)

    def start_load(k, carry):
        load(lax.rem(first + k, BLKS)).start()
        return carry

    lax.fori_loop(0, BLKS, start_load, 0)
    lab_copy = pltpu.make_async_copy(labels, lab, lab_sem)
    lab_copy.start()
    ids_copy = pltpu.make_async_copy(ids_hbm, ids, small_sem)
    ids_copy.start()

    barrier = pltpu.get_barrier_semaphore()
    for who in partners:
        pl.semaphore_signal(barrier, inc=1, device_id=who, device_id_type=MESH)

    stencil_weights(w)
    ids_copy.wait()
    count = counts[0]
    act = [jnp.where(s < count, 1.0, 0.0).astype(F32) for s in range(SLOTS)]

    e0f = e0.reshape((SLOTS + 2) * BLKS * ROWS, LANES)
    e1f = e1.reshape((SLOTS + 2) * BLKS * ROWS, LANES)
    u2f = u2.reshape(SLOTS * BLKS * ROWS, LANES)

    def edges(flat, step, j):
        for side, row in ((0, 0), (1, ROWS - 1)):
            for half in range(2):
                start = (SUB * half + 1) * STRIDE + j * ROWS + row
                hs[step, side, j, pl.ds(SUB * half, SUB), :] = flat[pl.ds(start, SUB, stride=STRIDE), :]

    def add_halo(flat, offset, step):
        def one(j, carry):
            for side, row in ((0, 0), (1, ROWS - 1)):
                for half in range(2):
                    start = (SUB * half + offset) * STRIDE + j * ROWS + row
                    where = pl.ds(start, SUB, stride=STRIDE)
                    flat[where, :] = flat[where, :] + 0.15 * hr[step, side, j, pl.ds(SUB * half, SUB), :]
            return carry
        lax.fori_loop(0, BLKS, one, 0)


    def core_send(rnd, h):
        return pltpu.make_async_remote_copy(
            p.at[rnd, pl.ds(HALF * (1 - h), HALF)], r1.at[rnd],
            send_sem.at[rnd, 0], recv_sem.at[rnd, 0], device_id=sibling, device_id_type=MESH)

    def chunk_at(h, x):
        return pl.ds(HALF * h + CHUNK * x, CHUNK)

    def x_send(rnd, h, d):
        return pltpu.make_async_remote_copy(
            p.at[rnd, chunk_at(h, lax.rem(xi + d, NX4))], r2.at[rnd, d - 1],
            send_sem.at[rnd, d], recv_sem.at[rnd, d], device_id=xpeer[d], device_id_type=MESH)

    def z_send(rnd):
        return pltpu.make_async_remote_copy(
            t.at[rnd], r3.at[rnd],
            send_sem.at[rnd, 4], recv_sem.at[rnd, 4], device_id=zpeer, device_id_type=MESH)

    def ag_send(rnd, h, total, d):
        own = total.at[chunk_at(h, xi)]
        return pltpu.make_async_remote_copy(
            own, own, send_sem.at[rnd, 4 + d], recv_sem.at[rnd, 4 + d],
            device_id=xpeer[d], device_id_type=MESH)

    def ag_recv(rnd, h, total, d):
        got = total.at[chunk_at(h, lax.rem(xi + NX4 - d, NX4))]
        return pltpu.make_async_remote_copy(
            got, got, send_sem.at[rnd, 4 + d], recv_sem.at[rnd, 4 + d],
            device_id=xpeer[d], device_id_type=MESH)

    def fwd(rnd, h, total, d):
        got = total.at[chunk_at(h, lax.rem(xi + NX4 - d, NX4))]
        return pltpu.make_async_remote_copy(
            got, got, send_sem.at[rnd, 8 + d], recv_sem.at[rnd, 8 + d],
            device_id=sibling, device_id_type=MESH)

    def halo(step, side):
        return pltpu.make_async_remote_copy(
            hs.at[step, side], hr.at[step, 1 - side],
            hsend.at[step, side], hrecv.at[step, 1 - side],
            device_id=before if side == 0 else after, device_id_type=MESH)

    def reduce_chunk(rnd, h, x):
        for i in range(CHUNK):
            k = CHUNK * x + i
            p[rnd, HALF * h + k] = p[rnd, HALF * h + k] + r1[rnd, k]

    def pass1(k, carry):
        j = lax.rem(first + k, BLKS)
        load(j).wait()
        acc = [jnp.zeros((2 * SUB, LANES), F32) for _ in range(TILES // 2)]
        for s in range(SLOTS):
            for r in range(TILES // 2):
                rows = pl.ds(2 * SUB * r, 2 * SUB)
                c = e0[s + 1, j, rows, :] * act[s]
                e0[s + 1, j, rows, :] = c
                acc[r] = acc[r] + c * c
                x[s, j, rows, :LANES], x[s, j, rows, LANES:] = split(c)
        for r in range(TILES // 2):
            p[0, j, pl.ds(2 * SUB * r, 2 * SUB), :] = acc[r]
        edges(e0f, 0, j)
        return carry

    lane = lax.broadcasted_iota(jnp.int32, (SUB, LANES), 1)
    sub = lax.broadcasted_iota(jnp.int32, (SUB, LANES), 0)
    low = lane < LANES // 2

    def planes(s, y):
        lhs = x[s].reshape(BLKS * ROWS, 2 * LANES)
        y[...] = jnp.dot(lhs, w[...], preferred_element_type=F32)

    def point(src, dst, dst_shift, s, y):
        gid = jnp.where(s < count, ids[s], -1)
        row = (s + 1) * STRIDE
        for j in range(BLKS):
            left = (j + BLKS - 1) % BLKS * ROWS
            right = (j + 1) % BLKS * ROWS
            for r in range(TILES):
                at = row + j * ROWS + SUB * r
                c = src[pl.ds(pl.multiple_of(at, SUB), SUB), :]
                up_x = src[pl.ds(at + 1, SUB), :]
                dn_x = src[pl.ds(at - 1, SUB), :]
                if r == TILES - 1:
                    up_x = jnp.where(sub == SUB - 1, 0.0, up_x)
                if r == 0:
                    dn_x = jnp.where(sub == 0, 0.0, dn_x)
                own = y[j * ROWS + SUB * r:j * ROWS + SUB * r + SUB, :LANES]
                spill = jnp.where(
                    low, y[left + SUB * r:left + SUB * r + SUB, LANES:],
                    y[right + SUB * r:right + SUB * r + SUB, LANES:])
                nb_sum = (up_x + dn_x) + (own + spill)
                labs = lab[pl.ds(SUB * r, SUB), j * LANES:j * LANES + LANES]
                mark = jnp.where(labs == gid, 0.15, 0.0).astype(F32)
                val = 0.15 * nb_sum + c * (0.175 + 0.15 * (c * c)) + mark
                dst[pl.ds(pl.multiple_of(at + dst_shift, SUB), SUB), :] = val

    def linear(src, dst, dst_shift, s_lo, s_hi):
        planes(s_lo, ya)

        def one(i, carry):
            s = s_lo + 2 * i
            planes(s + 1, yb)
            point(src, dst, dst_shift, s, ya)
            planes(jnp.minimum(s + 2, s_hi - 1), ya)
            point(src, dst, dst_shift, s + 1, yb)
            return carry

        lax.fori_loop(0, (s_hi - s_lo) // 2, one, 0)

    def pass2(k, carry):
        j = k
        tot = [0.225 * s1[j, pl.ds(2 * SUB * r, 2 * SUB), :] for r in range(TILES // 2)]
        acc = [jnp.zeros((2 * SUB, LANES), F32) for _ in range(TILES // 2)]
        for s in range(SLOTS):
            for r in range(TILES // 2):
                rows = pl.ds(2 * SUB * r, 2 * SUB)
                v = e1[s + 1, j, rows, :] - e0[s + 1, j, rows, :] * tot[r]
                e1[s + 1, j, rows, :] = v
                acc[r] = acc[r] + v * v
                x[s, j, rows, :LANES], x[s, j, rows, LANES:] = split(v)
        for r in range(TILES // 2):
            p[1, j, pl.ds(2 * SUB * r, 2 * SUB), :] = acc[r]
        edges(e1f, 1, j)
        return carry

    def exchange(rnd, h, total, seg, halo_step):
        core_send(rnd, h).wait_recv()
        for d in (2, 1, 3):
            reduce_chunk(rnd, h, lax.rem(xi + d, NX4))
            x_send(rnd, h, d).start()
        halo(halo_step, 0).start()
        halo(halo_step, 1).start()
        reduce_chunk(rnd, h, xi)
        seg(0)
        for d in (1, 3, 2):
            x_send(rnd, h, d).wait_recv()
        for i in range(CHUNK):
            mine = p[rnd, HALF * h + CHUNK * xi + i]
            t[rnd, i] = (mine + r2[rnd, 1, i]) + (r2[rnd, 0, i] + r2[rnd, 2, i])
        z_send(rnd).start()
        seg(1)
        z_send(rnd).wait_recv()
        for i in range(CHUNK):
            total[HALF * h + CHUNK * xi + i] = t[rnd, i] + r3[rnd, i]
        for d in (2, 1, 3):
            ag_send(rnd, h, total, d).start()
        fwd(rnd, h, total, 0).start()
        seg(2)
        for d in (1, 3, 2):
            ag_recv(rnd, h, total, d).wait_recv()
            fwd(rnd, h, total, d).start()

    def finish(rnd, h, total):
        for d in range(4):
            other = total.at[chunk_at(1 - h, lax.rem(xi + NX4 - d, NX4))]
            pltpu.make_async_remote_copy(
                other, other, send_sem.at[rnd, 8 + d], recv_sem.at[rnd, 8 + d],
                device_id=sibling, device_id_type=MESH).wait_recv()

    cuts = (0, 4, 10, 16)

    lax.fori_loop(0, HALF, pass1, 0)
    pl.semaphore_wait(barrier, len(partners))
    core_send(0, core).start()
    lax.fori_loop(HALF, BLKS, pass1, 0)
    lab_copy.wait()
    exchange(0, core, s1, lambda k: linear(e0f, e1f, 0, cuts[k], cuts[k + 1]), 0)
    halo(0, 0).wait_recv()
    halo(0, 1).wait_recv()
    add_halo(e1f, 1, 0)
    lax.fori_loop(HALF * core, HALF * core + HALF, pass2, 0)
    core_send(1, 1 - core).start()
    finish(0, core, s1)
    lax.fori_loop(HALF * (1 - core), HALF * (1 - core) + HALF, pass2, 0)
    exchange(1, 1 - core, s2, lambda k: linear(e1f, u2f, -STRIDE, cuts[k], cuts[k + 1]), 1)
    halo(1, 0).wait_recv()
    halo(1, 1).wait_recv()
    add_halo(u2f, 0, 1)
    finish(1, 1 - core, s2)

    for rnd, h, total in ((0, core, s1), (1, 1 - core, s2)):
        core_send(rnd, h).wait_send()
        for d in (1, 2, 3):
            x_send(rnd, h, d).wait_send()
            ag_send(rnd, h, total, d).wait_send()
        z_send(rnd).wait_send()
        for d in range(4):
            fwd(rnd, h, total, d).wait_send()
        for side in range(2):
            halo(rnd, side).wait_send()


def last(e1, u2, s2, out, stage, sem):
    def copy(s):
        return pltpu.make_async_copy(stage.at[s], out.at[s], sem.at[s])

    def one(s, carry):
        def blocks(j, carry):
            cols = pl.ds(pl.multiple_of(j * LANES, LANES), LANES)
            for r in range(TILES):
                rows = pl.ds(SUB * r, SUB)
                stage[s, rows, cols] = u2[s, j, rows, :] - e1[s + 1, j, rows, :] * (0.225 * s2[j, rows, :])
            return carry
        lax.fori_loop(0, BLKS, blocks, 0, unroll=4)
        copy(s).start()
        return carry

    lax.fori_loop(0, SLOTS, one, 0)

    def drain(s, carry):
        copy(s).wait()
        return carry
    lax.fori_loop(0, SLOTS, drain, 0)


def body(order, grain_ids, counts, labels):
    any_space = pl.BlockSpec(memory_space=pltpu.HBM)
    vmem = pl.BlockSpec(memory_space=pltpu.VMEM)
    grain_ids = pltpu.with_memory_space_constraint(grain_ids, pltpu.HBM)
    order = pltpu.with_memory_space_constraint(order, pltpu.HBM)
    labels = pltpu.with_memory_space_constraint(labels, pltpu.HBM)
    e1, u2, s2 = pl.pallas_call(
        kernel,
        out_shape=(
            pltpu.VMEM((SLOTS + 2, BLKS, ROWS, LANES), F32),
            pltpu.VMEM((SLOTS, BLKS, ROWS, LANES), F32),
            pltpu.VMEM((BLKS, ROWS, LANES), F32),
        ),
        in_specs=[any_space, any_space, pl.BlockSpec(memory_space=pltpu.SMEM), any_space],
        out_specs=(vmem, vmem, vmem),
        scratch_shapes=[
            pltpu.SMEM((SLOTS,), jnp.int32),
            pltpu.VMEM((2 * LANES, 2 * LANES), jnp.bfloat16),
            pltpu.VMEM((SLOTS, BLKS, ROWS, 2 * LANES), jnp.bfloat16),
            pltpu.VMEM((BLKS * ROWS, 2 * LANES), F32),
            pltpu.VMEM((BLKS * ROWS, 2 * LANES), F32),
            pltpu.VMEM((SLOTS + 2, BLKS, ROWS, LANES), F32),
            pltpu.VMEM((ROWS, BLKS * LANES), jnp.int32),
            pltpu.VMEM((2, BLKS, ROWS, LANES), F32),
            pltpu.VMEM((2, HALF, ROWS, LANES), F32),
            pltpu.VMEM((2, 3, CHUNK, ROWS, LANES), F32),
            pltpu.VMEM((2, CHUNK, ROWS, LANES), F32),
            pltpu.VMEM((2, CHUNK, ROWS, LANES), F32),
            pltpu.VMEM((BLKS, ROWS, LANES), F32),
            pltpu.VMEM((2, 2, BLKS, SLOTS, LANES), F32),
            pltpu.VMEM((2, 2, BLKS, SLOTS, LANES), F32),
            pltpu.SemaphoreType.DMA((BLKS,)),
            pltpu.SemaphoreType.DMA,
            pltpu.SemaphoreType.DMA,
            pltpu.SemaphoreType.DMA((2, 12)),
            pltpu.SemaphoreType.DMA((2, 12)),
            pltpu.SemaphoreType.DMA((2, 2)),
            pltpu.SemaphoreType.DMA((2, 2)),
        ],
        compiler_params=pltpu.CompilerParams(
            collective_id=0, has_side_effects=True, vmem_limit_bytes=32 * 1024 * 1024),
        name="steps",
    )(order, grain_ids, counts, labels)
    return pl.pallas_call(
        last,
        out_shape=jax.ShapeDtypeStruct(order.shape, F32),
        in_specs=[vmem, vmem, vmem],
        out_specs=any_space,
        scratch_shapes=[
            pltpu.VMEM((SLOTS, ROWS, BLKS * LANES), F32),
            pltpu.SemaphoreType.DMA((SLOTS,)),
        ],
        compiler_params=pltpu.CompilerParams(vmem_limit_bytes=32 * 1024 * 1024),
        name="last",
    )(e1, u2, s2)


def solution(mesh):
    placed = (P("grain", "blk", None), P("grain"), P("grain"), P("blk", None))
    return jax.shard_map(
        body, mesh=mesh, in_specs=placed, out_specs=P("grain", "blk", None), check_vma=False
    )
```

```python
import jax
import jax.numpy as jnp
from jax import lax
from jax.experimental import pallas as pl
from jax.experimental.pallas import tpu as pltpu
from jax.sharding import PartitionSpec as P

NZ = 32
LANES = 128
SUB = 8
PAIR = 2 * SUB
SLOTS = 16
ROWS = 32
BLKS = 16
HALF = BLKS // 2
CHUNK = 2
NX4 = 4
TILES = ROWS // SUB
STRIDE = BLKS * ROWS
MESH = pl.DeviceIdType.MESH
F32 = jnp.float32
BF16 = jnp.bfloat16

NAMES = (
    ["core_s", "core_pq", "core_e"]
    + [f"x_{a}{d}" for a in ("s", "pq", "e") for d in (1, 2, 3)]
    + [f"all_{a}{z}{d}" for a in ("s", "t") for z in (0, 1) for d in range(4) if z + d]
    + [f"fwd_{a}{d}" for a in ("s", "t") for d in range(4)]
    + [f"halo_{a}{side}" for a in ("eta", "u", "s") for side in (0, 1)]
)
INDEX = {name: i for i, name in enumerate(NAMES)}


def stencil_weights(w):
    k = lax.rem(lax.broadcasted_iota(jnp.int32, (2 * LANES, 2 * LANES), 0), LANES)
    n = lax.broadcasted_iota(jnp.int32, (2 * LANES, 2 * LANES), 1)
    m = lax.rem(n, LANES)
    same_y = lax.div(k, NZ) == lax.div(m, NZ)
    dz = lax.rem(m - k + LANES, NZ)
    z_side = same_y & ((dz == 1) | (dz == NZ - 1))
    y_side = (m - k == NZ) | (k - m == NZ)
    wrap = (m - k == LANES - NZ) | (k - m == LANES - NZ)
    inside = jnp.where(z_side, 1.0, 0.0) + jnp.where(y_side, 1.0, 0.0)
    w[...] = jnp.where(n < LANES, inside, jnp.where(wrap, 1.0, 0.0)).astype(BF16)


def split(c):
    hi = c.astype(BF16)
    lo = (c - hi.astype(F32)).astype(BF16)
    return hi, lo


def kernel(order, ids_hbm, counts, labels, e1, u2, s2, ids, w, x, ya, yb, e0, lab,
           ps, pq, pe, r1s, r1pq, r1e, r2s, r2pq, r2e, part_s, part_t, s1,
           h_eta, g_eta, h_u, g_u, h_s, g_s,
           load_sem, lab_sem, small_sem, send_sem, recv_sem):
    b = lax.axis_index("blk")
    g = lax.axis_index("grain")
    nb = lax.axis_size("blk")
    core = lax.rem(g, 2)
    xi = lax.rem(lax.div(g, 2), NX4)
    zh = lax.div(g, 2 * NX4)

    def grain(z, d, c):
        return (b, (z * NX4 + lax.rem(xi + d, NX4)) * 2 + c)

    sibling = grain(zh, 0, 1 - core)
    peer = {(z, d): grain(zh if z == 0 else 1 - zh, d, core)
            for z in (0, 1) for d in range(4) if z + d}
    after = (lax.rem(b + 1, nb), g)
    before = (lax.rem(b + nb - 1, nb), g)
    toward = (before, after)
    partners = [sibling, after, before] + list(peer.values())

    def remote(name, src, dst, who):
        i = INDEX[name]
        return pltpu.make_async_remote_copy(
            src, dst, send_sem.at[i], recv_sem.at[i], device_id=who, device_id_type=MESH)

    def load(j):
        cols = pl.ds(pl.multiple_of(j * LANES, LANES), LANES)
        return pltpu.make_async_copy(order.at[:, :, cols], e0.at[pl.ds(1, SLOTS), j], load_sem.at[j])

    mine = HALF * core
    theirs = HALF * (1 - core)

    def start_load(k, carry):
        load(lax.rem(theirs + k, BLKS)).start()
        return carry

    lax.fori_loop(0, BLKS, start_load, 0)
    ids_copy = pltpu.make_async_copy(ids_hbm, ids, small_sem)
    ids_copy.start()
    lab_copy = pltpu.make_async_copy(labels, lab, lab_sem)
    lab_copy.start()

    barrier = pltpu.get_barrier_semaphore()
    for who in partners:
        pl.semaphore_signal(barrier, inc=1, device_id=who, device_id_type=MESH)

    stencil_weights(w)
    count = counts[0]
    act = [jnp.where(s < count, 1.0, 0.0).astype(F32) for s in range(SLOTS)]

    e0f = e0.reshape((SLOTS + 2) * STRIDE, LANES)
    e1f = e1.reshape((SLOTS + 2) * STRIDE, LANES)
    u2f = u2.reshape(SLOTS * STRIDE, LANES)
    sub = lax.broadcasted_iota(jnp.int32, (SUB, LANES), 0)
    lane = lax.broadcasted_iota(jnp.int32, (SUB, LANES), 1)
    low = lane < LANES // 2
    edge_row = (0, ROWS - 1)

    def at_edge(offset, j, side, half):
        start = (SUB * half + offset) * STRIDE + j * ROWS + edge_row[side]
        return pl.ds(start, SUB, stride=STRIDE)

    def slots_of(half):
        return pl.ds(SUB * half, SUB)

    def chunk(d):
        return pl.ds(mine + CHUNK * lax.rem(xi + NX4 + d, NX4), CHUNK)

    def local(d):
        return CHUNK * lax.rem(xi + NX4 + d, NX4)


    def core_s():
        return remote("core_s", ps.at[pl.ds(theirs, HALF)], r1s, sibling)

    def core_pq():
        return remote("core_pq", pq.at[pl.ds(theirs, HALF)], r1pq, sibling)

    def core_e():
        return remote("core_e", pe.at[pl.ds(theirs, HALF)], r1e, sibling)

    def x_s(d):
        return remote(f"x_s{d}", ps.at[chunk(d)], r2s.at[d - 1], peer[0, d])

    def x_pq(d):
        return remote(f"x_pq{d}", pq.at[chunk(d)], r2pq.at[d - 1], peer[0, d])

    def x_e(d):
        return remote(f"x_e{d}", pe.at[chunk(d)], r2e.at[d - 1], peer[0, d])

    def spread(a, part, z, d, got=False):
        return remote(f"all_{a}{z}{d}", part.at[0, chunk(0)], part.at[z, chunk(-d if got else 0)], peer[z, d])

    def forward(a, total, d, got=False):
        where = chunk(-d)
        if got:
            where = pl.ds(theirs + local(-d), CHUNK)
        return remote(f"fwd_{a}{d}", total.at[where], total.at[where], sibling)

    def halo(a, src, dst, side):
        return remote(f"halo_{a}{side}", src.at[side], dst.at[1 - side], toward[side])

    far_first = ((1, 2), (1, 1), (1, 3), (1, 0), (0, 2), (0, 1), (0, 3))

    def add_chunk(total, got, d):
        for i in range(CHUNK):
            k = local(d) + i
            total[mine + k] = total[mine + k] + got[k]

    def first_pass(k, carry):
        j = lax.rem(theirs + k, BLKS)
        load(j).wait()
        acc = [jnp.zeros((PAIR, LANES), F32) for _ in range(TILES // 2)]
        for s in range(SLOTS):
            for r in range(TILES // 2):
                rows = pl.ds(PAIR * r, PAIR)
                c = e0[s + 1, j, rows, :] * act[s]
                e0[s + 1, j, rows, :] = c
                acc[r] = acc[r] + c * c
                x[s, j, rows, :LANES], x[s, j, rows, LANES:] = split(c)
        for r in range(TILES // 2):
            ps[j, pl.ds(PAIR * r, PAIR), :] = acc[r]
        for side in range(2):
            for half in range(2):
                h_eta[side, j, slots_of(half), :] = e0f[at_edge(1, j, side, half), :]
        return carry

    def planes(s, y):
        lhs = x[s].reshape(BLKS * ROWS, 2 * LANES)
        y[...] = jnp.dot(lhs, w[...], preferred_element_type=F32)

    def point(src, dst, dst_shift, s, y):
        gid = jnp.where(s < count, ids[s], -1)
        row = (s + 1) * STRIDE
        for j in range(BLKS):
            left = (j + BLKS - 1) % BLKS * ROWS
            right = (j + 1) % BLKS * ROWS
            for r in range(TILES):
                at = row + j * ROWS + SUB * r
                c = src[pl.ds(pl.multiple_of(at, SUB), SUB), :]
                up_x = src[pl.ds(at + 1, SUB), :]
                dn_x = src[pl.ds(at - 1, SUB), :]
                if r == TILES - 1:
                    up_x = jnp.where(sub == SUB - 1, 0.0, up_x)
                if r == 0:
                    dn_x = jnp.where(sub == 0, 0.0, dn_x)
                own = y[j * ROWS + SUB * r:j * ROWS + SUB * r + SUB, :LANES]
                spill = jnp.where(
                    low, y[left + SUB * r:left + SUB * r + SUB, LANES:],
                    y[right + SUB * r:right + SUB * r + SUB, LANES:])
                nb_sum = (up_x + dn_x) + (own + spill)
                labs = lab[pl.ds(SUB * r, SUB), j * LANES:j * LANES + LANES]
                mark = jnp.where(labs == gid, 0.15, 0.0).astype(F32)
                val = 0.15 * nb_sum + c * (0.175 + 0.15 * (c * c)) + mark
                dst[pl.ds(pl.multiple_of(at + dst_shift, SUB), SUB), :] = val

    def linear(src, dst, dst_shift, s_lo, s_hi):
        planes(s_lo, ya)

        def one(i, carry):
            s = s_lo + 2 * i
            planes(s + 1, yb)
            point(src, dst, dst_shift, s, ya)
            planes(jnp.minimum(s + 2, s_hi - 1), ya)
            point(src, dst, dst_shift, s + 1, yb)
            return carry

        lax.fori_loop(0, (s_hi - s_lo) // 2, one, 0)

    def sums_pass(j, carry):
        accp = [jnp.zeros((SUB, LANES), F32) for _ in range(TILES)]
        accq = [jnp.zeros((SUB, LANES), F32) for _ in range(TILES)]
        for s in range(SLOTS):
            for r in range(TILES):
                rows = pl.ds(SUB * r, SUB)
                u = e1[s + 1, j, rows, :]
                accp[r] = accp[r] + u * e0[s + 1, j, rows, :]
                accq[r] = accq[r] + u * u
        for r in range(TILES):
            pq[j, 0, pl.ds(SUB * r, SUB), :] = accp[r]
            pq[j, 1, pl.ds(SUB * r, SUB), :] = accq[r]
        return carry

    def edge_pass(j, carry):
        fix = jnp.zeros((SUB, LANES), F32)
        for side in range(2):
            dp = jnp.zeros((SUB, LANES), F32)
            dq = jnp.zeros((SUB, LANES), F32)
            for half in range(2):
                where = at_edge(1, j, side, half)
                add = 0.15 * g_eta[side, j, slots_of(half), :]
                old = e1f[where, :]
                new = old + add
                e1f[where, :] = new
                h_u[side, j, slots_of(half), :] = new
                dp = dp + add * h_eta[side, j, slots_of(half), :]
                dq = dq + add * (old + new)
            fix = jnp.where(sub == side, jnp.sum(dp, axis=0, keepdims=True), fix)
            fix = jnp.where(sub == side + 2, jnp.sum(dq, axis=0, keepdims=True), fix)
        pe[j] = fix
        return carry

    def second_pass(j, carry):
        tot = [0.225 * s1[j, pl.ds(PAIR * r, PAIR), :] for r in range(TILES // 2)]
        for s in range(SLOTS):
            for r in range(TILES // 2):
                rows = pl.ds(PAIR * r, PAIR)
                v = e1[s + 1, j, rows, :] - e0[s + 1, j, rows, :] * tot[r]
                e1[s + 1, j, rows, :] = v
                x[s, j, rows, :LANES], x[s, j, rows, LANES:] = split(v)
        return carry

    def last_edge_pass(j, carry):
        for side in range(2):
            tot = 0.225 * g_s[side, pl.ds(j, 1), :]
            for half in range(2):
                where = at_edge(0, j, side, half)
                out = g_u[side, j, slots_of(half), :] - g_eta[side, j, slots_of(half), :] * tot
                u2f[where, :] = u2f[where, :] + 0.15 * out
        return carry

    lax.fori_loop(0, HALF, first_pass, 0)
    pl.semaphore_wait(barrier, len(partners))
    core_s().start()
    lax.fori_loop(HALF, BLKS, first_pass, 0)
    for side in range(2):
        halo("eta", h_eta, g_eta, side).start()
    ids_copy.wait()
    lab_copy.wait()
    linear(e0f, e1f, 0, 0, 4)

    core_s().wait_recv()
    for d in (2, 1, 3):
        add_chunk(ps, r1s, d)
        x_s(d).start()
    add_chunk(ps, r1s, 0)
    linear(e0f, e1f, 0, 4, SLOTS)

    lax.fori_loop(theirs, theirs + HALF, sums_pass, 0)
    core_pq().start()
    lax.fori_loop(mine, mine + HALF, sums_pass, 0)

    for d in (1, 3, 2):
        x_s(d).wait_recv()
    for i in range(CHUNK):
        k = mine + local(0) + i
        part_s[0, k] = (ps[k] + r2s[1, i]) + (r2s[0, i] + r2s[2, i])
    for z, d in far_first:
        spread("s", part_s, z, d).start()

    core_pq().wait_recv()
    for d in (2, 1, 3):
        add_chunk(pq, r1pq, d)
        x_pq(d).start()
    add_chunk(pq, r1pq, 0)

    for side in range(2):
        halo("eta", h_eta, g_eta, side).wait_recv()
    lax.fori_loop(theirs, theirs + HALF, edge_pass, 0)
    core_e().start()
    lax.fori_loop(mine, mine + HALF, edge_pass, 0)
    for side in range(2):
        halo("u", h_u, g_u, side).start()
    core_e().wait_recv()
    for d in (2, 1, 3):
        add_chunk(pe, r1e, d)
        x_e(d).start()
    add_chunk(pe, r1e, 0)

    def total_s(d):
        spread("s", part_s, 1, d, True).wait_recv()
        if d:
            spread("s", part_s, 0, d, True).wait_recv()
        for i in range(CHUNK):
            k = mine + local(-d) + i
            s1[k] = part_s[0, k] + part_s[1, k]
        forward("s", s1, d).start()

    def total_t(d):
        spread("t", part_t, 1, d, True).wait_recv()
        if d:
            spread("t", part_t, 0, d, True).wait_recv()
        for i in range(CHUNK):
            k = mine + local(-d) + i
            s = s1[k]
            s2[k] = (part_t[0, k] + part_t[1, k]) + 0.050625 * (s * s * s)
        forward("t", s2, d).start()

    total_s(0)
    for d in (1, 3, 2):
        x_pq(d).wait_recv()
    for d in (1, 3, 2):
        x_e(d).wait_recv()
    for i in range(CHUNK):
        k = mine + local(0) + i
        s = 0.45 * s1[k]
        p_sum = (pq[k, 0] + r2pq[1, i, 0]) + (r2pq[0, i, 0] + r2pq[2, i, 0])
        q_sum = (pq[k, 1] + r2pq[1, i, 1]) + (r2pq[0, i, 1] + r2pq[2, i, 1])
        part_t[0, k] = q_sum - s * p_sum
        fix = (pe[k] + r2e[1, i]) + (r2e[0, i] + r2e[2, i])
        for side, row in enumerate(edge_row):
            part_t[0, k, row:row + 1, :] = part_t[0, k, row:row + 1, :] + (
                fix[side + 2:side + 3] - 0.45 * s1[k, row:row + 1, :] * fix[side:side + 1])
    for z, d in far_first:
        spread("t", part_t, z, d).start()

    for d in (1, 3, 2):
        total_s(d)
    lax.fori_loop(mine, mine + HALF, second_pass, 0)
    for d in range(4):
        forward("s", s1, d, True).wait_recv()
    for side, row in enumerate(edge_row):
        for j in range(BLKS):
            h_s[side, j:j + 1, :] = s1[j, row:row + 1, :]
        halo("s", h_s, g_s, side).start()
    lax.fori_loop(theirs, theirs + HALF, second_pass, 0)
    linear(e1f, u2f, -STRIDE, 0, 12)

    for d in (0, 1, 3, 2):
        total_t(d)
    linear(e1f, u2f, -STRIDE, 12, SLOTS)
    for side in range(2):
        halo("u", h_u, g_u, side).wait_recv()
        halo("s", h_s, g_s, side).wait_recv()
    lax.fori_loop(0, BLKS, last_edge_pass, 0)
    for d in range(4):
        forward("t", s2, d, True).wait_recv()

    core_s().wait_send()
    core_pq().wait_send()
    core_e().wait_send()
    for d in (1, 2, 3):
        x_s(d).wait_send()
        x_pq(d).wait_send()
        x_e(d).wait_send()
    for z, d in far_first:
        spread("s", part_s, z, d).wait_send()
        spread("t", part_t, z, d).wait_send()
    for d in range(4):
        forward("s", s1, d).wait_send()
        forward("t", s2, d).wait_send()
    for side in range(2):
        halo("eta", h_eta, g_eta, side).wait_send()
        halo("u", h_u, g_u, side).wait_send()
        halo("s", h_s, g_s, side).wait_send()


def last(e1, u2, s2, out, stage, sem):
    def copy(s):
        return pltpu.make_async_copy(stage.at[s], out.at[s], sem.at[s])

    def one(s, carry):
        def blocks(j, carry):
            cols = pl.ds(pl.multiple_of(j * LANES, LANES), LANES)
            for r in range(TILES):
                rows = pl.ds(SUB * r, SUB)
                stage[s, rows, cols] = u2[s, j, rows, :] - e1[s + 1, j, rows, :] * (0.225 * s2[j, rows, :])
            return carry
        lax.fori_loop(0, BLKS, blocks, 0, unroll=4)
        copy(s).start()
        return carry

    lax.fori_loop(0, SLOTS, one, 0)

    def drain(s, carry):
        copy(s).wait()
        return carry
    lax.fori_loop(0, SLOTS, drain, 0)


def body(order, grain_ids, counts, labels):
    hbm = pl.BlockSpec(memory_space=pltpu.HBM)
    smem = pl.BlockSpec(memory_space=pltpu.SMEM)
    vmem = pl.BlockSpec(memory_space=pltpu.VMEM)
    grain_ids = pltpu.with_memory_space_constraint(grain_ids, pltpu.HBM)
    order = pltpu.with_memory_space_constraint(order, pltpu.HBM)
    labels = pltpu.with_memory_space_constraint(labels, pltpu.HBM)

    def f32(*shape):
        return pltpu.VMEM(shape, F32)

    e1, u2, s2 = pl.pallas_call(
        kernel,
        out_shape=(
            f32(SLOTS + 2, BLKS, ROWS, LANES),
            f32(SLOTS, BLKS, ROWS, LANES),
            f32(BLKS, ROWS, LANES),
        ),
        in_specs=[hbm, hbm, smem, hbm],
        out_specs=(vmem, vmem, vmem),
        scratch_shapes=[
            pltpu.SMEM((SLOTS,), jnp.int32),
            pltpu.VMEM((2 * LANES, 2 * LANES), BF16),
            pltpu.VMEM((SLOTS, BLKS, ROWS, 2 * LANES), BF16),
            f32(BLKS * ROWS, 2 * LANES),
            f32(BLKS * ROWS, 2 * LANES),
            f32(SLOTS + 2, BLKS, ROWS, LANES),
            pltpu.VMEM((ROWS, BLKS * LANES), jnp.int32),
            f32(BLKS, ROWS, LANES),
            f32(BLKS, 2, ROWS, LANES),
            f32(BLKS, SUB, LANES),
            f32(HALF, ROWS, LANES),
            f32(HALF, 2, ROWS, LANES),
            f32(HALF, SUB, LANES),
            f32(3, CHUNK, ROWS, LANES),
            f32(3, CHUNK, 2, ROWS, LANES),
            f32(3, CHUNK, SUB, LANES),
            f32(2, BLKS, ROWS, LANES),
            f32(2, BLKS, ROWS, LANES),
            f32(BLKS, ROWS, LANES),
            f32(2, BLKS, SLOTS, LANES),
            f32(2, BLKS, SLOTS, LANES),
            f32(2, BLKS, SLOTS, LANES),
            f32(2, BLKS, SLOTS, LANES),
            f32(2, BLKS, LANES),
            f32(2, BLKS, LANES),
            pltpu.SemaphoreType.DMA((BLKS,)),
            pltpu.SemaphoreType.DMA,
            pltpu.SemaphoreType.DMA,
            pltpu.SemaphoreType.DMA((len(NAMES),)),
            pltpu.SemaphoreType.DMA((len(NAMES),)),
        ],
        compiler_params=pltpu.CompilerParams(
            collective_id=0, has_side_effects=True, vmem_limit_bytes=40 * 1024 * 1024),
        name="steps",
    )(order, grain_ids, counts, labels)
    return pl.pallas_call(
        last,
        out_shape=jax.ShapeDtypeStruct(order.shape, F32),
        in_specs=[vmem, vmem, vmem],
        out_specs=hbm,
        scratch_shapes=[
            pltpu.VMEM((SLOTS, ROWS, BLKS * LANES), F32),
            pltpu.SemaphoreType.DMA((SLOTS,)),
        ],
        compiler_params=pltpu.CompilerParams(vmem_limit_bytes=32 * 1024 * 1024),
        name="last",
    )(e1, u2, s2)


def solution(mesh):
    placed = (P("grain", "blk", None), P("grain"), P("grain"), P("blk", None))
    return jax.shard_map(
        body, mesh=mesh, in_specs=placed, out_specs=P("grain", "blk", None), check_vma=False
    )
```

```python
import jax
import jax.numpy as jnp
from jax import lax
from jax.experimental import pallas as pl
from jax.experimental.pallas import tpu as pltpu
from jax.sharding import PartitionSpec as P

NZ = 32
LANES = 128
SUB = 8
PAIR = 2 * SUB
SLOTS = 16
ROWS = 32
BLKS = 16
HALF = BLKS // 2
CHUNK = 2
NX4 = 4
TILES = ROWS // SUB
STRIDE = BLKS * ROWS
MESH = pl.DeviceIdType.MESH
F32 = jnp.float32
BF16 = jnp.bfloat16

NAMES = (
    ["core_s", "core_pq", "core_e"]
    + [f"x_{a}{d}" for a in ("s", "pq", "e") for d in (1, 2, 3)]
    + [f"z_{a}" for a in ("s", "t")]
    + [f"all_{a}{d}" for a in ("s", "t") for d in (1, 2, 3)]
    + [f"fwd_{a}{d}" for a in ("s", "t") for d in range(4)]
    + [f"halo_{a}{side}" for a in ("eta", "u", "s") for side in (0, 1)]
)
INDEX = {name: i for i, name in enumerate(NAMES)}


def stencil_weights(w):
    k = lax.rem(lax.broadcasted_iota(jnp.int32, (2 * LANES, 2 * LANES), 0), LANES)
    n = lax.broadcasted_iota(jnp.int32, (2 * LANES, 2 * LANES), 1)
    m = lax.rem(n, LANES)
    same_y = lax.div(k, NZ) == lax.div(m, NZ)
    dz = lax.rem(m - k + LANES, NZ)
    z_side = same_y & ((dz == 1) | (dz == NZ - 1))
    y_side = (m - k == NZ) | (k - m == NZ)
    wrap = (m - k == LANES - NZ) | (k - m == LANES - NZ)
    inside = jnp.where(z_side, 1.0, 0.0) + jnp.where(y_side, 1.0, 0.0)
    w[...] = jnp.where(n < LANES, inside, jnp.where(wrap, 1.0, 0.0)).astype(BF16)


def split(c):
    hi = c.astype(BF16)
    lo = (c - hi.astype(F32)).astype(BF16)
    return hi, lo


def kernel(order, ids_hbm, counts, labels, e1, u2, s2, ids, w, x, ya, yb, e0, lab,
           ps, pq, pe, r1s, r1pq, r1e, r2s, r2pq, r2e, part_s, part_t, z_s, z_t, s1,
           h_eta, g_eta, h_u, g_u, h_s, g_s,
           load_sem, lab_sem, small_sem, send_sem, recv_sem):
    b = lax.axis_index("blk")
    g = lax.axis_index("grain")
    nb = lax.axis_size("blk")
    core = lax.rem(g, 2)
    xi = lax.rem(lax.div(g, 2), NX4)
    zh = lax.div(g, 2 * NX4)

    def grain(z, d, c):
        return (b, (z * NX4 + lax.rem(xi + d, NX4)) * 2 + c)

    sibling = grain(zh, 0, 1 - core)
    across = grain(1 - zh, 0, core)
    peer = {d: grain(zh, d, core) for d in (1, 2, 3)}
    after = (lax.rem(b + 1, nb), g)
    before = (lax.rem(b + nb - 1, nb), g)
    toward = (before, after)
    partners = [sibling, across, after, before] + list(peer.values())

    def remote(name, src, dst, who):
        i = INDEX[name]
        return pltpu.make_async_remote_copy(
            src, dst, send_sem.at[i], recv_sem.at[i], device_id=who, device_id_type=MESH)

    def load(j):
        cols = pl.ds(pl.multiple_of(j * LANES, LANES), LANES)
        return pltpu.make_async_copy(order.at[:, :, cols], e0.at[pl.ds(1, SLOTS), j], load_sem.at[j])

    mine = HALF * core
    theirs = HALF * (1 - core)

    def start_load(k, carry):
        load(lax.rem(theirs + k, BLKS)).start()
        return carry

    lax.fori_loop(0, BLKS, start_load, 0)
    ids_copy = pltpu.make_async_copy(ids_hbm, ids, small_sem)
    ids_copy.start()
    lab_copy = pltpu.make_async_copy(labels, lab, lab_sem)
    lab_copy.start()

    barrier = pltpu.get_barrier_semaphore()
    for who in partners:
        pl.semaphore_signal(barrier, inc=1, device_id=who, device_id_type=MESH)

    stencil_weights(w)
    count = counts[0]
    act = [jnp.where(s < count, 1.0, 0.0).astype(F32) for s in range(SLOTS)]

    e0f = e0.reshape((SLOTS + 2) * STRIDE, LANES)
    e1f = e1.reshape((SLOTS + 2) * STRIDE, LANES)
    u2f = u2.reshape(SLOTS * STRIDE, LANES)
    sub = lax.broadcasted_iota(jnp.int32, (SUB, LANES), 0)
    lane = lax.broadcasted_iota(jnp.int32, (SUB, LANES), 1)
    low = lane < LANES // 2
    edge_row = (0, ROWS - 1)

    def at_edge(offset, j, side, half):
        start = (SUB * half + offset) * STRIDE + j * ROWS + edge_row[side]
        return pl.ds(start, SUB, stride=STRIDE)

    def slots_of(half):
        return pl.ds(SUB * half, SUB)

    def chunk(d):
        return pl.ds(mine + CHUNK * lax.rem(xi + NX4 + d, NX4), CHUNK)

    def local(d):
        return CHUNK * lax.rem(xi + NX4 + d, NX4)


    def core_s():
        return remote("core_s", ps.at[pl.ds(theirs, HALF)], r1s, sibling)

    def core_pq():
        return remote("core_pq", pq.at[pl.ds(theirs, HALF)], r1pq, sibling)

    def core_e():
        return remote("core_e", pe.at[pl.ds(theirs, HALF)], r1e, sibling)

    def x_s(d):
        return remote(f"x_s{d}", ps.at[chunk(d)], r2s.at[d - 1], peer[d])

    def x_pq(d):
        return remote(f"x_pq{d}", pq.at[chunk(d)], r2pq.at[d - 1], peer[d])

    def x_e(d):
        return remote(f"x_e{d}", pe.at[chunk(d)], r2e.at[d - 1], peer[d])

    def z_swap(a, part, got):
        return remote(f"z_{a}", part, got, across)

    def gather(a, total, d, got=False):
        where = chunk(-d if got else 0)
        return remote(f"all_{a}{d}", total.at[where], total.at[where], peer[d])

    def forward(a, total, d, got=False):
        where = chunk(-d)
        if got:
            where = pl.ds(theirs + local(-d), CHUNK)
        return remote(f"fwd_{a}{d}", total.at[where], total.at[where], sibling)

    def halo(a, src, dst, side):
        return remote(f"halo_{a}{side}", src.at[side], dst.at[1 - side], toward[side])

    def add_chunk(total, got, d):
        for i in range(CHUNK):
            k = local(d) + i
            total[mine + k] = total[mine + k] + got[k]

    def first_pass(k, carry):
        j = lax.rem(theirs + k, BLKS)
        load(j).wait()
        acc = [jnp.zeros((PAIR, LANES), F32) for _ in range(TILES // 2)]
        for s in range(SLOTS):
            for r in range(TILES // 2):
                rows = pl.ds(PAIR * r, PAIR)
                c = e0[s + 1, j, rows, :] * act[s]
                e0[s + 1, j, rows, :] = c
                acc[r] = acc[r] + c * c
                x[s, j, rows, :LANES], x[s, j, rows, LANES:] = split(c)
        for r in range(TILES // 2):
            ps[j, pl.ds(PAIR * r, PAIR), :] = acc[r]
        for side in range(2):
            for half in range(2):
                h_eta[side, j, slots_of(half), :] = e0f[at_edge(1, j, side, half), :]
        return carry

    def planes(s, y):
        lhs = x[s].reshape(BLKS * ROWS, 2 * LANES)
        y[...] = jnp.dot(lhs, w[...], preferred_element_type=F32)

    def point(src, dst, dst_shift, s, y):
        gid = jnp.where(s < count, ids[s], -1)
        row = (s + 1) * STRIDE
        for j in range(BLKS):
            left = (j + BLKS - 1) % BLKS * ROWS
            right = (j + 1) % BLKS * ROWS
            for r in range(TILES):
                at = row + j * ROWS + SUB * r
                c = src[pl.ds(pl.multiple_of(at, SUB), SUB), :]
                up_x = src[pl.ds(at + 1, SUB), :]
                dn_x = src[pl.ds(at - 1, SUB), :]
                if r == TILES - 1:
                    up_x = jnp.where(sub == SUB - 1, 0.0, up_x)
                if r == 0:
                    dn_x = jnp.where(sub == 0, 0.0, dn_x)
                own = y[j * ROWS + SUB * r:j * ROWS + SUB * r + SUB, :LANES]
                spill = jnp.where(
                    low, y[left + SUB * r:left + SUB * r + SUB, LANES:],
                    y[right + SUB * r:right + SUB * r + SUB, LANES:])
                nb_sum = (up_x + dn_x) + (own + spill)
                labs = lab[pl.ds(SUB * r, SUB), j * LANES:j * LANES + LANES]
                mark = jnp.where(labs == gid, 0.15, 0.0).astype(F32)
                val = 0.15 * nb_sum + c * (0.175 + 0.15 * (c * c)) + mark
                dst[pl.ds(pl.multiple_of(at + dst_shift, SUB), SUB), :] = val

    def linear(src, dst, dst_shift, s_lo, s_hi):
        planes(s_lo, ya)

        def one(i, carry):
            s = s_lo + 2 * i
            planes(s + 1, yb)
            point(src, dst, dst_shift, s, ya)
            planes(jnp.minimum(s + 2, s_hi - 1), ya)
            point(src, dst, dst_shift, s + 1, yb)
            return carry

        lax.fori_loop(0, (s_hi - s_lo) // 2, one, 0)

    def sums_pass(j, carry):
        accp = [jnp.zeros((SUB, LANES), F32) for _ in range(TILES)]
        accq = [jnp.zeros((SUB, LANES), F32) for _ in range(TILES)]
        for s in range(SLOTS):
            for r in range(TILES):
                rows = pl.ds(SUB * r, SUB)
                u = e1[s + 1, j, rows, :]
                accp[r] = accp[r] + u * e0[s + 1, j, rows, :]
                accq[r] = accq[r] + u * u
        for r in range(TILES):
            pq[j, 0, pl.ds(SUB * r, SUB), :] = accp[r]
            pq[j, 1, pl.ds(SUB * r, SUB), :] = accq[r]
        return carry

    def edge_pass(j, carry):
        fix = jnp.zeros((SUB, LANES), F32)
        for side in range(2):
            dp = jnp.zeros((SUB, LANES), F32)
            dq = jnp.zeros((SUB, LANES), F32)
            for half in range(2):
                where = at_edge(1, j, side, half)
                add = 0.15 * g_eta[side, j, slots_of(half), :]
                old = e1f[where, :]
                new = old + add
                e1f[where, :] = new
                h_u[side, j, slots_of(half), :] = new
                dp = dp + add * h_eta[side, j, slots_of(half), :]
                dq = dq + add * (old + new)
            fix = jnp.where(sub == side, jnp.sum(dp, axis=0, keepdims=True), fix)
            fix = jnp.where(sub == side + 2, jnp.sum(dq, axis=0, keepdims=True), fix)
        pe[j] = fix
        return carry

    def second_pass(j, carry):
        tot = [0.225 * s1[j, pl.ds(PAIR * r, PAIR), :] for r in range(TILES // 2)]
        for s in range(SLOTS):
            for r in range(TILES // 2):
                rows = pl.ds(PAIR * r, PAIR)
                v = e1[s + 1, j, rows, :] - e0[s + 1, j, rows, :] * tot[r]
                e1[s + 1, j, rows, :] = v
                x[s, j, rows, :LANES], x[s, j, rows, LANES:] = split(v)
        return carry

    def last_edge_pass(j, carry):
        for side in range(2):
            tot = 0.225 * g_s[side, pl.ds(j, 1), :]
            for half in range(2):
                where = at_edge(0, j, side, half)
                out = g_u[side, j, slots_of(half), :] - g_eta[side, j, slots_of(half), :] * tot
                u2f[where, :] = u2f[where, :] + 0.15 * out
        return carry

    lax.fori_loop(0, HALF, first_pass, 0)
    pl.semaphore_wait(barrier, len(partners))
    core_s().start()
    lax.fori_loop(HALF, BLKS, first_pass, 0)
    for side in range(2):
        halo("eta", h_eta, g_eta, side).start()
    ids_copy.wait()
    lab_copy.wait()
    linear(e0f, e1f, 0, 0, 4)

    core_s().wait_recv()
    for d in (2, 1, 3):
        add_chunk(ps, r1s, d)
        x_s(d).start()
    add_chunk(ps, r1s, 0)
    linear(e0f, e1f, 0, 4, SLOTS)

    lax.fori_loop(theirs, theirs + HALF, sums_pass, 0)
    core_pq().start()
    lax.fori_loop(mine, mine + HALF, sums_pass, 0)

    for d in (1, 3, 2):
        x_s(d).wait_recv()
    for i in range(CHUNK):
        k = mine + local(0) + i
        part_s[i] = (ps[k] + r2s[1, i]) + (r2s[0, i] + r2s[2, i])
    z_swap("s", part_s, z_s).start()

    core_pq().wait_recv()
    for d in (2, 1, 3):
        add_chunk(pq, r1pq, d)
        x_pq(d).start()
    add_chunk(pq, r1pq, 0)

    for side in range(2):
        halo("eta", h_eta, g_eta, side).wait_recv()
    lax.fori_loop(0, HALF, lambda k, c: edge_pass(theirs + k, c), 0, unroll=True)
    core_e().start()
    lax.fori_loop(0, HALF, lambda k, c: edge_pass(mine + k, c), 0, unroll=True)
    for side in range(2):
        halo("u", h_u, g_u, side).start()
    core_e().wait_recv()
    for d in (2, 1, 3):
        add_chunk(pe, r1e, d)
        x_e(d).start()
    add_chunk(pe, r1e, 0)

    z_swap("s", part_s, z_s).wait_recv()
    for i in range(CHUNK):
        s1[mine + local(0) + i] = part_s[i] + z_s[i]
    for d in (2, 1, 3):
        gather("s", s1, d).start()
    forward("s", s1, 0).start()

    for d in (1, 3, 2):
        x_pq(d).wait_recv()
    for d in (1, 3, 2):
        x_e(d).wait_recv()
    for i in range(CHUNK):
        k = mine + local(0) + i
        s = 0.45 * s1[k]
        p_sum = (pq[k, 0] + r2pq[1, i, 0]) + (r2pq[0, i, 0] + r2pq[2, i, 0])
        q_sum = (pq[k, 1] + r2pq[1, i, 1]) + (r2pq[0, i, 1] + r2pq[2, i, 1])
        part_t[i] = q_sum - s * p_sum
        fix = (pe[k] + r2e[1, i]) + (r2e[0, i] + r2e[2, i])
        for side, row in enumerate(edge_row):
            part_t[i, row:row + 1, :] = part_t[i, row:row + 1, :] + (
                fix[side + 2:side + 3] - 0.45 * s1[k, row:row + 1, :] * fix[side:side + 1])
    z_swap("t", part_t, z_t).start()

    for d in (1, 3, 2):
        gather("s", s1, d, True).wait_recv()
        forward("s", s1, d).start()
    lax.fori_loop(mine, mine + HALF, second_pass, 0)

    z_swap("t", part_t, z_t).wait_recv()
    for i in range(CHUNK):
        k = mine + local(0) + i
        s = s1[k]
        s2[k] = (part_t[i] + z_t[i]) + 0.050625 * (s * s * s)
    for d in (2, 1, 3):
        gather("t", s2, d).start()
    forward("t", s2, 0).start()

    for d in range(4):
        forward("s", s1, d, True).wait_recv()
    for side, row in enumerate(edge_row):
        for j in range(BLKS):
            h_s[side, j:j + 1, :] = s1[j, row:row + 1, :]
        halo("s", h_s, g_s, side).start()
    lax.fori_loop(theirs, theirs + HALF, second_pass, 0)
    linear(e1f, u2f, -STRIDE, 0, 12)

    for d in (1, 3, 2):
        gather("t", s2, d, True).wait_recv()
        forward("t", s2, d).start()
    linear(e1f, u2f, -STRIDE, 12, SLOTS)
    for side in range(2):
        halo("u", h_u, g_u, side).wait_recv()
        halo("s", h_s, g_s, side).wait_recv()
    lax.fori_loop(0, BLKS, last_edge_pass, 0, unroll=8)
    for d in range(4):
        forward("t", s2, d, True).wait_recv()

    core_s().wait_send()
    core_pq().wait_send()
    core_e().wait_send()
    for d in (1, 2, 3):
        x_s(d).wait_send()
        x_pq(d).wait_send()
        x_e(d).wait_send()
        gather("s", s1, d).wait_send()
        gather("t", s2, d).wait_send()
    z_swap("s", part_s, z_s).wait_send()
    z_swap("t", part_t, z_t).wait_send()
    for d in range(4):
        forward("s", s1, d).wait_send()
        forward("t", s2, d).wait_send()
    for side in range(2):
        halo("eta", h_eta, g_eta, side).wait_send()
        halo("u", h_u, g_u, side).wait_send()
        halo("s", h_s, g_s, side).wait_send()


def last(e1, u2, s2, out, stage, sem):
    def copy(s):
        return pltpu.make_async_copy(stage.at[s], out.at[s], sem.at[s])

    def one(s, carry):
        def blocks(j, carry):
            cols = pl.ds(pl.multiple_of(j * LANES, LANES), LANES)
            for r in range(TILES):
                rows = pl.ds(SUB * r, SUB)
                stage[s, rows, cols] = u2[s, j, rows, :] - e1[s + 1, j, rows, :] * (0.225 * s2[j, rows, :])
            return carry
        lax.fori_loop(0, BLKS, blocks, 0, unroll=4)
        copy(s).start()
        return carry

    lax.fori_loop(0, SLOTS, one, 0)

    def drain(s, carry):
        copy(s).wait()
        return carry
    lax.fori_loop(0, SLOTS, drain, 0)


def body(order, grain_ids, counts, labels):
    hbm = pl.BlockSpec(memory_space=pltpu.HBM)
    smem = pl.BlockSpec(memory_space=pltpu.SMEM)
    vmem = pl.BlockSpec(memory_space=pltpu.VMEM)
    grain_ids = pltpu.with_memory_space_constraint(grain_ids, pltpu.HBM)
    order = pltpu.with_memory_space_constraint(order, pltpu.HBM)
    labels = pltpu.with_memory_space_constraint(labels, pltpu.HBM)

    def f32(*shape):
        return pltpu.VMEM(shape, F32)

    e1, u2, s2 = pl.pallas_call(
        kernel,
        out_shape=(
            f32(SLOTS + 2, BLKS, ROWS, LANES),
            f32(SLOTS, BLKS, ROWS, LANES),
            f32(BLKS, ROWS, LANES),
        ),
        in_specs=[hbm, hbm, smem, hbm],
        out_specs=(vmem, vmem, vmem),
        scratch_shapes=[
            pltpu.SMEM((SLOTS,), jnp.int32),
            pltpu.VMEM((2 * LANES, 2 * LANES), BF16),
            pltpu.VMEM((SLOTS, BLKS, ROWS, 2 * LANES), BF16),
            f32(BLKS * ROWS, 2 * LANES),
            f32(BLKS * ROWS, 2 * LANES),
            f32(SLOTS + 2, BLKS, ROWS, LANES),
            pltpu.VMEM((ROWS, BLKS * LANES), jnp.int32),
            f32(BLKS, ROWS, LANES),
            f32(BLKS, 2, ROWS, LANES),
            f32(BLKS, SUB, LANES),
            f32(HALF, ROWS, LANES),
            f32(HALF, 2, ROWS, LANES),
            f32(HALF, SUB, LANES),
            f32(3, CHUNK, ROWS, LANES),
            f32(3, CHUNK, 2, ROWS, LANES),
            f32(3, CHUNK, SUB, LANES),
            f32(CHUNK, ROWS, LANES),
            f32(CHUNK, ROWS, LANES),
            f32(CHUNK, ROWS, LANES),
            f32(CHUNK, ROWS, LANES),
            f32(BLKS, ROWS, LANES),
            f32(2, BLKS, SLOTS, LANES),
            f32(2, BLKS, SLOTS, LANES),
            f32(2, BLKS, SLOTS, LANES),
            f32(2, BLKS, SLOTS, LANES),
            f32(2, BLKS, LANES),
            f32(2, BLKS, LANES),
            pltpu.SemaphoreType.DMA((BLKS,)),
            pltpu.SemaphoreType.DMA,
            pltpu.SemaphoreType.DMA,
            pltpu.SemaphoreType.DMA((len(NAMES),)),
            pltpu.SemaphoreType.DMA((len(NAMES),)),
        ],
        compiler_params=pltpu.CompilerParams(
            collective_id=0, has_side_effects=True, vmem_limit_bytes=40 * 1024 * 1024),
        name="steps",
    )(order, grain_ids, counts, labels)
    return pl.pallas_call(
        last,
        out_shape=jax.ShapeDtypeStruct(order.shape, F32),
        in_specs=[vmem, vmem, vmem],
        out_specs=hbm,
        scratch_shapes=[
            pltpu.VMEM((SLOTS, ROWS, BLKS * LANES), F32),
            pltpu.SemaphoreType.DMA((SLOTS,)),
        ],
        compiler_params=pltpu.CompilerParams(vmem_limit_bytes=32 * 1024 * 1024),
        name="last",
    )(e1, u2, s2)


def solution(mesh):
    placed = (P("grain", "blk", None), P("grain"), P("grain"), P("blk", None))
    return jax.shard_map(
        body, mesh=mesh, in_specs=placed, out_specs=P("grain", "blk", None), check_vma=False
    )
```

```python
import jax
import jax.numpy as jnp
from jax import lax
from jax.experimental import pallas as pl
from jax.experimental.pallas import tpu as pltpu
from jax.sharding import PartitionSpec as P

NZ = 32
LANES = 128
SUB = 8
PAIR = 2 * SUB
SLOTS = 16
ROWS = 32
BLKS = 16
HALF = BLKS // 2
CHUNK = 2
NX4 = 4
TILES = ROWS // SUB
STRIDE = BLKS * ROWS
MESH = pl.DeviceIdType.MESH
F32 = jnp.float32
BF16 = jnp.bfloat16

NAMES = (
    ["core_s", "core_pq", "core_e"]
    + [f"x_{a}{d}" for a in ("s", "pq", "e") for d in (1, 2, 3)]
    + [f"z_{a}" for a in ("s", "t")]
    + [f"all_{a}{d}" for a in ("s", "t") for d in (1, 2, 3)]
    + [f"fwd_{a}{d}" for a in ("s", "t") for d in range(4)]
    + [f"halo_{a}{side}" for a in ("eta", "u", "s") for side in (0, 1)]
)
INDEX = {name: i for i, name in enumerate(NAMES)}


def stencil_weights(w):
    k = lax.rem(lax.broadcasted_iota(jnp.int32, (2 * LANES, 2 * LANES), 0), LANES)
    n = lax.broadcasted_iota(jnp.int32, (2 * LANES, 2 * LANES), 1)
    m = lax.rem(n, LANES)
    same_y = lax.div(k, NZ) == lax.div(m, NZ)
    dz = lax.rem(m - k + LANES, NZ)
    z_side = same_y & ((dz == 1) | (dz == NZ - 1))
    y_side = (m - k == NZ) | (k - m == NZ)
    wrap = (m - k == LANES - NZ) | (k - m == LANES - NZ)
    inside = jnp.where(z_side, 1.0, 0.0) + jnp.where(y_side, 1.0, 0.0)
    w[...] = jnp.where(n < LANES, inside, jnp.where(wrap, 1.0, 0.0)).astype(BF16)


def split(c):
    hi = c.astype(BF16)
    lo = (c - hi.astype(F32)).astype(BF16)
    return hi, lo


def kernel(order, ids_hbm, counts, labels, e1, u2, s2, ids, w, x, ya, yb, e0, lab,
           ps, pq, pe, r1s, r1pq, r1e, r2s, r2pq, r2e, part_s, part_t, z_s, z_t, s1,
           h_eta, g_eta, h_u, g_u, h_s, g_s,
           load_sem, lab_sem, small_sem, send_sem, recv_sem):
    b = lax.axis_index("blk")
    g = lax.axis_index("grain")
    nb = lax.axis_size("blk")
    core = lax.rem(g, 2)
    xi = lax.rem(lax.div(g, 2), NX4)
    zh = lax.div(g, 2 * NX4)

    def grain(z, d, c):
        return (b, (z * NX4 + lax.rem(xi + d, NX4)) * 2 + c)

    sibling = grain(zh, 0, 1 - core)
    across = grain(1 - zh, 0, core)
    peer = {d: grain(zh, d, core) for d in (1, 2, 3)}
    after = (lax.rem(b + 1, nb), g)
    before = (lax.rem(b + nb - 1, nb), g)
    toward = (before, after)
    partners = [sibling, across, after, before] + list(peer.values())

    def remote(name, src, dst, who):
        i = INDEX[name]
        return pltpu.make_async_remote_copy(
            src, dst, send_sem.at[i], recv_sem.at[i], device_id=who, device_id_type=MESH)

    def load(j):
        cols = pl.ds(pl.multiple_of(j * LANES, LANES), LANES)
        return pltpu.make_async_copy(order.at[:, :, cols], e0.at[pl.ds(1, SLOTS), j], load_sem.at[j])

    mine = HALF * core
    theirs = HALF * (1 - core)

    def start_load(k, carry):
        load(lax.rem(theirs + k, BLKS)).start()
        return carry

    barrier = pltpu.get_barrier_semaphore()
    for who in partners:
        pl.semaphore_signal(barrier, inc=1, device_id=who, device_id_type=MESH)

    lax.fori_loop(0, BLKS, start_load, 0)
    ids_copy = pltpu.make_async_copy(ids_hbm, ids, small_sem)
    ids_copy.start()
    lab_copy = pltpu.make_async_copy(labels, lab, lab_sem)
    lab_copy.start()

    stencil_weights(w)
    count = counts[0]
    act = [jnp.where(s < count, 1.0, 0.0).astype(F32) for s in range(SLOTS)]

    e0f = e0.reshape((SLOTS + 2) * STRIDE, LANES)
    e1f = e1.reshape((SLOTS + 2) * STRIDE, LANES)
    u2f = u2.reshape(SLOTS * STRIDE, LANES)
    sub = lax.broadcasted_iota(jnp.int32, (SUB, LANES), 0)
    lane = lax.broadcasted_iota(jnp.int32, (SUB, LANES), 1)
    low = lane < LANES // 2
    edge_row = (0, ROWS - 1)

    def at_edge(offset, j, side, half):
        start = (SUB * half + offset) * STRIDE + j * ROWS + edge_row[side]
        return pl.ds(start, SUB, stride=STRIDE)

    def slots_of(half):
        return pl.ds(SUB * half, SUB)

    def chunk(d):
        return pl.ds(mine + CHUNK * lax.rem(xi + NX4 + d, NX4), CHUNK)

    def local(d):
        return CHUNK * lax.rem(xi + NX4 + d, NX4)


    def core_s():
        return remote("core_s", ps.at[pl.ds(theirs, HALF)], r1s, sibling)

    def core_pq():
        return remote("core_pq", pq.at[pl.ds(theirs, HALF)], r1pq, sibling)

    def core_e():
        return remote("core_e", pe.at[pl.ds(theirs, HALF)], r1e, sibling)

    def x_s(d):
        return remote(f"x_s{d}", ps.at[chunk(d)], r2s.at[d - 1], peer[d])

    def x_pq(d):
        return remote(f"x_pq{d}", pq.at[chunk(d)], r2pq.at[d - 1], peer[d])

    def x_e(d):
        return remote(f"x_e{d}", pe.at[chunk(d)], r2e.at[d - 1], peer[d])

    def z_swap(a, part, got):
        return remote(f"z_{a}", part, got, across)

    def gather(a, total, d, got=False):
        where = chunk(-d if got else 0)
        return remote(f"all_{a}{d}", total.at[where], total.at[where], peer[d])

    def forward(a, total, d, got=False):
        where = chunk(-d)
        if got:
            where = pl.ds(theirs + local(-d), CHUNK)
        return remote(f"fwd_{a}{d}", total.at[where], total.at[where], sibling)

    def halo(a, src, dst, side):
        return remote(f"halo_{a}{side}", src.at[side], dst.at[1 - side], toward[side])

    def add_chunk(total, got, d):
        for i in range(CHUNK):
            k = local(d) + i
            total[mine + k] = total[mine + k] + got[k]

    def first_pass(k, carry):
        j = lax.rem(theirs + k, BLKS)
        load(j).wait()
        acc = [jnp.zeros((PAIR, LANES), F32) for _ in range(TILES // 2)]
        for s in range(SLOTS):
            for r in range(TILES // 2):
                rows = pl.ds(PAIR * r, PAIR)
                c = e0[s + 1, j, rows, :] * act[s]
                e0[s + 1, j, rows, :] = c
                acc[r] = acc[r] + c * c
                x[s, j, rows, :LANES], x[s, j, rows, LANES:] = split(c)
        for r in range(TILES // 2):
            ps[j, pl.ds(PAIR * r, PAIR), :] = acc[r]
        for side in range(2):
            for half in range(2):
                h_eta[side, j, slots_of(half), :] = e0f[at_edge(1, j, side, half), :]
        return carry

    def planes(s, y):
        lhs = x[s].reshape(BLKS * ROWS, 2 * LANES)
        y[...] = jnp.dot(lhs, w[...], preferred_element_type=F32)

    def point(src, dst, dst_shift, s, y):
        gid = jnp.where(s < count, ids[s], -1)
        row = (s + 1) * STRIDE
        for j in range(BLKS):
            left = (j + BLKS - 1) % BLKS * ROWS
            right = (j + 1) % BLKS * ROWS
            for r in range(TILES):
                at = row + j * ROWS + SUB * r
                c = src[pl.ds(pl.multiple_of(at, SUB), SUB), :]
                up_x = src[pl.ds(at + 1, SUB), :]
                dn_x = src[pl.ds(at - 1, SUB), :]
                if r == TILES - 1:
                    up_x = jnp.where(sub == SUB - 1, 0.0, up_x)
                if r == 0:
                    dn_x = jnp.where(sub == 0, 0.0, dn_x)
                own = y[j * ROWS + SUB * r:j * ROWS + SUB * r + SUB, :LANES]
                spill = jnp.where(
                    low, y[left + SUB * r:left + SUB * r + SUB, LANES:],
                    y[right + SUB * r:right + SUB * r + SUB, LANES:])
                nb_sum = (up_x + dn_x) + (own + spill)
                labs = lab[pl.ds(SUB * r, SUB), j * LANES:j * LANES + LANES]
                mark = jnp.where(labs == gid, 0.15, 0.0).astype(F32)
                val = 0.15 * nb_sum + c * (0.175 + 0.15 * (c * c)) + mark
                dst[pl.ds(pl.multiple_of(at + dst_shift, SUB), SUB), :] = val

    def linear(src, dst, dst_shift, s_lo, s_hi):
        planes(s_lo, ya)

        def one(i, carry):
            s = s_lo + 2 * i
            planes(s + 1, yb)
            point(src, dst, dst_shift, s, ya)
            planes(jnp.minimum(s + 2, SLOTS - 1), ya)
            point(src, dst, dst_shift, s + 1, yb)
            return carry

        lax.fori_loop(0, lax.div(s_hi - s_lo, 2), one, 0)

    def sums_pass(j, carry):
        accp = [jnp.zeros((SUB, LANES), F32) for _ in range(TILES)]
        accq = [jnp.zeros((SUB, LANES), F32) for _ in range(TILES)]
        for s in range(SLOTS):
            for r in range(TILES):
                rows = pl.ds(SUB * r, SUB)
                u = e1[s + 1, j, rows, :]
                accp[r] = accp[r] + u * e0[s + 1, j, rows, :]
                accq[r] = accq[r] + u * u
        for r in range(TILES):
            pq[j, 0, pl.ds(SUB * r, SUB), :] = accp[r]
            pq[j, 1, pl.ds(SUB * r, SUB), :] = accq[r]
        return carry

    def edge_pass(j, carry):
        fix = jnp.zeros((SUB, LANES), F32)
        for side in range(2):
            dp = jnp.zeros((SUB, LANES), F32)
            dq = jnp.zeros((SUB, LANES), F32)
            for half in range(2):
                where = at_edge(1, j, side, half)
                add = 0.15 * g_eta[side, j, slots_of(half), :]
                old = e1f[where, :]
                new = old + add
                e1f[where, :] = new
                h_u[side, j, slots_of(half), :] = new
                dp = dp + add * h_eta[side, j, slots_of(half), :]
                dq = dq + add * (old + new)
            fix = jnp.where(sub == side, jnp.sum(dp, axis=0, keepdims=True), fix)
            fix = jnp.where(sub == side + 2, jnp.sum(dq, axis=0, keepdims=True), fix)
        pe[j] = fix
        return carry

    def second_pass(j, carry):
        tot = [0.225 * s1[j, pl.ds(PAIR * r, PAIR), :] for r in range(TILES // 2)]
        for s in range(SLOTS):
            for r in range(TILES // 2):
                rows = pl.ds(PAIR * r, PAIR)
                v = e1[s + 1, j, rows, :] - e0[s + 1, j, rows, :] * tot[r]
                e1[s + 1, j, rows, :] = v
                x[s, j, rows, :LANES], x[s, j, rows, LANES:] = split(v)
        return carry

    def last_edge_pass(j, carry):
        for side in range(2):
            tot = 0.225 * g_s[side, pl.ds(j, 1), :]
            for half in range(2):
                where = at_edge(0, j, side, half)
                out = g_u[side, j, slots_of(half), :] - g_eta[side, j, slots_of(half), :] * tot
                u2f[where, :] = u2f[where, :] + 0.15 * out
        return carry

    lax.fori_loop(0, BLKS, first_pass, 0)
    ids_copy.wait()
    lab_copy.wait()
    linear(e0f, e1f, 0, 0, 4)
    pl.semaphore_wait(barrier, len(partners))
    core_s().start()
    for side in range(2):
        halo("eta", h_eta, g_eta, side).start()
    linear(e0f, e1f, 0, 4, 4 + 4)

    core_s().wait_recv()
    for d in (2, 1, 3):
        add_chunk(ps, r1s, d)
        x_s(d).start()
    add_chunk(ps, r1s, 0)
    linear(e0f, e1f, 0, 4 + 4, SLOTS)

    lax.fori_loop(theirs, theirs + HALF, sums_pass, 0)
    core_pq().start()
    lax.fori_loop(mine, mine + HALF, sums_pass, 0)

    for d in (1, 3, 2):
        x_s(d).wait_recv()
    for i in range(CHUNK):
        k = mine + local(0) + i
        part_s[i] = (ps[k] + r2s[1, i]) + (r2s[0, i] + r2s[2, i])
    z_swap("s", part_s, z_s).start()

    core_pq().wait_recv()
    for d in (2, 1, 3):
        add_chunk(pq, r1pq, d)
        x_pq(d).start()
    add_chunk(pq, r1pq, 0)

    for side in range(2):
        halo("eta", h_eta, g_eta, side).wait_recv()
    lax.fori_loop(0, HALF, lambda k, c: edge_pass(theirs + k, c), 0, unroll=True)
    core_e().start()
    lax.fori_loop(0, HALF, lambda k, c: edge_pass(mine + k, c), 0, unroll=True)
    for side in range(2):
        halo("u", h_u, g_u, side).start()
    core_e().wait_recv()
    for d in (2, 1, 3):
        add_chunk(pe, r1e, d)
        x_e(d).start()
    add_chunk(pe, r1e, 0)

    z_swap("s", part_s, z_s).wait_recv()
    for i in range(CHUNK):
        s1[mine + local(0) + i] = part_s[i] + z_s[i]
    for d in (2, 1, 3):
        gather("s", s1, d).start()
    forward("s", s1, 0).start()

    for d in (1, 3, 2):
        x_pq(d).wait_recv()
    for d in (1, 3, 2):
        x_e(d).wait_recv()
    for i in range(CHUNK):
        k = mine + local(0) + i
        s = 0.45 * s1[k]
        p_sum = (pq[k, 0] + r2pq[1, i, 0]) + (r2pq[0, i, 0] + r2pq[2, i, 0])
        q_sum = (pq[k, 1] + r2pq[1, i, 1]) + (r2pq[0, i, 1] + r2pq[2, i, 1])
        part_t[i] = q_sum - s * p_sum
        fix = (pe[k] + r2e[1, i]) + (r2e[0, i] + r2e[2, i])
        for side, row in enumerate(edge_row):
            part_t[i, row:row + 1, :] = part_t[i, row:row + 1, :] + (
                fix[side + 2:side + 3] - 0.45 * s1[k, row:row + 1, :] * fix[side:side + 1])
    z_swap("t", part_t, z_t).start()

    for d in (1, 3, 2):
        gather("s", s1, d, True).wait_recv()
        forward("s", s1, d).start()
    lax.fori_loop(mine, mine + HALF, second_pass, 0)

    z_swap("t", part_t, z_t).wait_recv()
    for i in range(CHUNK):
        k = mine + local(0) + i
        s = s1[k]
        s2[k] = (part_t[i] + z_t[i]) + 0.050625 * (s * s * s)
    for d in (2, 1, 3):
        gather("t", s2, d).start()
    forward("t", s2, 0).start()

    for d in range(4):
        forward("s", s1, d, True).wait_recv()
    for side, row in enumerate(edge_row):
        for j in range(BLKS):
            h_s[side, j:j + 1, :] = s1[j, row:row + 1, :]
        halo("s", h_s, g_s, side).start()
    lax.fori_loop(theirs, theirs + HALF, second_pass, 0)
    linear(e1f, u2f, -STRIDE, 0, 12)

    for d in (1, 3, 2):
        gather("t", s2, d, True).wait_recv()
        forward("t", s2, d).start()
    linear(e1f, u2f, -STRIDE, 12, SLOTS)
    for side in range(2):
        halo("u", h_u, g_u, side).wait_recv()
        halo("s", h_s, g_s, side).wait_recv()
    lax.fori_loop(0, BLKS, last_edge_pass, 0, unroll=8)
    for d in range(4):
        forward("t", s2, d, True).wait_recv()

    core_s().wait_send()
    core_pq().wait_send()
    core_e().wait_send()
    for d in (1, 2, 3):
        x_s(d).wait_send()
        x_pq(d).wait_send()
        x_e(d).wait_send()
        gather("s", s1, d).wait_send()
        gather("t", s2, d).wait_send()
    z_swap("s", part_s, z_s).wait_send()
    z_swap("t", part_t, z_t).wait_send()
    for d in range(4):
        forward("s", s1, d).wait_send()
        forward("t", s2, d).wait_send()
    for side in range(2):
        halo("eta", h_eta, g_eta, side).wait_send()
        halo("u", h_u, g_u, side).wait_send()
        halo("s", h_s, g_s, side).wait_send()


def last(e1, u2, s2, out, stage, sem):
    def copy(s):
        return pltpu.make_async_copy(stage.at[s], out.at[s], sem.at[s])

    def one(s, carry):
        def blocks(j, carry):
            cols = pl.ds(pl.multiple_of(j * LANES, LANES), LANES)
            for r in range(TILES):
                rows = pl.ds(SUB * r, SUB)
                stage[s, rows, cols] = u2[s, j, rows, :] - e1[s + 1, j, rows, :] * (0.225 * s2[j, rows, :])
            return carry
        lax.fori_loop(0, BLKS, blocks, 0, unroll=4)
        copy(s).start()
        return carry

    lax.fori_loop(0, SLOTS, one, 0)

    def drain(s, carry):
        copy(s).wait()
        return carry
    lax.fori_loop(0, SLOTS, drain, 0)


def body(order, grain_ids, counts, labels):
    hbm = pl.BlockSpec(memory_space=pltpu.HBM)
    smem = pl.BlockSpec(memory_space=pltpu.SMEM)
    vmem = pl.BlockSpec(memory_space=pltpu.VMEM)
    grain_ids = pltpu.with_memory_space_constraint(grain_ids, pltpu.HBM)
    order = pltpu.with_memory_space_constraint(order, pltpu.HBM)
    labels = pltpu.with_memory_space_constraint(labels, pltpu.HBM)

    def f32(*shape):
        return pltpu.VMEM(shape, F32)

    e1, u2, s2 = pl.pallas_call(
        kernel,
        out_shape=(
            f32(SLOTS + 2, BLKS, ROWS, LANES),
            f32(SLOTS, BLKS, ROWS, LANES),
            f32(BLKS, ROWS, LANES),
        ),
        in_specs=[hbm, hbm, smem, hbm],
        out_specs=(vmem, vmem, vmem),
        scratch_shapes=[
            pltpu.SMEM((SLOTS,), jnp.int32),
            pltpu.VMEM((2 * LANES, 2 * LANES), BF16),
            pltpu.VMEM((SLOTS, BLKS, ROWS, 2 * LANES), BF16),
            f32(BLKS * ROWS, 2 * LANES),
            f32(BLKS * ROWS, 2 * LANES),
            f32(SLOTS + 2, BLKS, ROWS, LANES),
            pltpu.VMEM((ROWS, BLKS * LANES), jnp.int32),
            f32(BLKS, ROWS, LANES),
            f32(BLKS, 2, ROWS, LANES),
            f32(BLKS, SUB, LANES),
            f32(HALF, ROWS, LANES),
            f32(HALF, 2, ROWS, LANES),
            f32(HALF, SUB, LANES),
            f32(3, CHUNK, ROWS, LANES),
            f32(3, CHUNK, 2, ROWS, LANES),
            f32(3, CHUNK, SUB, LANES),
            f32(CHUNK, ROWS, LANES),
            f32(CHUNK, ROWS, LANES),
            f32(CHUNK, ROWS, LANES),
            f32(CHUNK, ROWS, LANES),
            f32(BLKS, ROWS, LANES),
            f32(2, BLKS, SLOTS, LANES),
            f32(2, BLKS, SLOTS, LANES),
            f32(2, BLKS, SLOTS, LANES),
            f32(2, BLKS, SLOTS, LANES),
            f32(2, BLKS, LANES),
            f32(2, BLKS, LANES),
            pltpu.SemaphoreType.DMA((BLKS,)),
            pltpu.SemaphoreType.DMA,
            pltpu.SemaphoreType.DMA,
            pltpu.SemaphoreType.DMA((len(NAMES),)),
            pltpu.SemaphoreType.DMA((len(NAMES),)),
        ],
        compiler_params=pltpu.CompilerParams(
            collective_id=0, has_side_effects=True, vmem_limit_bytes=40 * 1024 * 1024),
        name="steps",
    )(order, grain_ids, counts, labels)
    return pl.pallas_call(
        last,
        out_shape=jax.ShapeDtypeStruct(order.shape, F32),
        in_specs=[vmem, vmem, vmem],
        out_specs=hbm,
        scratch_shapes=[
            pltpu.VMEM((SLOTS, ROWS, BLKS * LANES), F32),
            pltpu.SemaphoreType.DMA((SLOTS,)),
        ],
        compiler_params=pltpu.CompilerParams(vmem_limit_bytes=32 * 1024 * 1024),
        name="last",
    )(e1, u2, s2)


def solution(mesh):
    placed = (P("grain", "blk", None), P("grain"), P("grain"), P("blk", None))
    return jax.shard_map(
        body, mesh=mesh, in_specs=placed, out_specs=P("grain", "blk", None), check_vma=False
    )
```

```python
import jax
import jax.numpy as jnp
from jax import lax
from jax.experimental import pallas as pl
from jax.experimental.pallas import tpu as pltpu
from jax.sharding import PartitionSpec as P

NZ = 32
LANES = 128
SUB = 8
PAIR = 2 * SUB
SLOTS = 16
ROWS = 32
BLKS = 16
HALF = BLKS // 2
CHUNK = 2
NX4 = 4
TILES = ROWS // SUB
STRIDE = BLKS * ROWS
MESH = pl.DeviceIdType.MESH
F32 = jnp.float32
BF16 = jnp.bfloat16

NAMES = (
    ["core_s", "core_pq", "core_e"]
    + [f"x_{a}{d}" for a in ("s", "pq", "e") for d in (1, 2, 3)]
    + [f"z_{a}" for a in ("s", "t")]
    + [f"all_{a}{d}" for a in ("s", "t") for d in (1, 2, 3)]
    + [f"fwd_{a}{d}" for a in ("s", "t") for d in range(4)]
    + [f"halo_{a}{side}" for a in ("eta", "u", "s") for side in (0, 1)]
)
INDEX = {name: i for i, name in enumerate(NAMES)}


def stencil_weights(w):
    k = lax.rem(lax.broadcasted_iota(jnp.int32, (2 * LANES, 2 * LANES), 0), LANES)
    n = lax.broadcasted_iota(jnp.int32, (2 * LANES, 2 * LANES), 1)
    m = lax.rem(n, LANES)
    same_y = lax.div(k, NZ) == lax.div(m, NZ)
    dz = lax.rem(m - k + LANES, NZ)
    z_side = same_y & ((dz == 1) | (dz == NZ - 1))
    y_side = (m - k == NZ) | (k - m == NZ)
    wrap = (m - k == LANES - NZ) | (k - m == LANES - NZ)
    inside = jnp.where(z_side, 1.0, 0.0) + jnp.where(y_side, 1.0, 0.0)
    w[...] = jnp.where(n < LANES, inside, jnp.where(wrap, 1.0, 0.0)).astype(BF16)


def split(c):
    hi = c.astype(BF16)
    lo = (c - hi.astype(F32)).astype(BF16)
    return hi, lo


def kernel(order, ids_hbm, counts, labels, e1, u2, s2, ids, w, x, ya, yb, e0, lab,
           ps, pq, pe, r1s, r1pq, r1e, r2s, r2pq, r2e, part_s, part_t, z_s, z_t, s1,
           h_eta, g_eta, h_u, g_u, h_s, g_s,
           load_sem, lab_sem, small_sem, send_sem, recv_sem):
    b = lax.axis_index("blk")
    g = lax.axis_index("grain")
    nb = lax.axis_size("blk")
    core = lax.rem(g, 2)
    xi = lax.rem(lax.div(g, 2), NX4)
    zh = lax.div(g, 2 * NX4)

    def grain(z, d, c):
        return (b, (z * NX4 + lax.rem(xi + d, NX4)) * 2 + c)

    sibling = grain(zh, 0, 1 - core)
    across = grain(1 - zh, 0, core)
    peer = {d: grain(zh, d, core) for d in (1, 2, 3)}
    after = (lax.rem(b + 1, nb), g)
    before = (lax.rem(b + nb - 1, nb), g)
    toward = (before, after)
    partners = [sibling, across, after, before] + list(peer.values())

    def remote(name, src, dst, who):
        i = INDEX[name]
        return pltpu.make_async_remote_copy(
            src, dst, send_sem.at[i], recv_sem.at[i], device_id=who, device_id_type=MESH)

    def load(j):
        cols = pl.ds(pl.multiple_of(j * LANES, LANES), LANES)
        return pltpu.make_async_copy(order.at[:, :, cols], e0.at[pl.ds(1, SLOTS), j], load_sem.at[j])

    mine = HALF * core
    theirs = HALF * (1 - core)

    def start_load(k, carry):
        load(lax.rem(theirs + k, BLKS)).start()
        return carry

    barrier = pltpu.get_barrier_semaphore()
    for who in partners:
        pl.semaphore_signal(barrier, inc=1, device_id=who, device_id_type=MESH)

    lax.fori_loop(0, BLKS, start_load, 0)
    ids_copy = pltpu.make_async_copy(ids_hbm, ids, small_sem)
    ids_copy.start()
    lab_copy = pltpu.make_async_copy(labels, lab, lab_sem)
    lab_copy.start()

    stencil_weights(w)
    count = counts[0]
    act = [jnp.where(s < count, 1.0, 0.0).astype(F32) for s in range(SLOTS)]

    e0f = e0.reshape((SLOTS + 2) * STRIDE, LANES)
    e1f = e1.reshape((SLOTS + 2) * STRIDE, LANES)
    u2f = u2.reshape((SLOTS + 1) * STRIDE, LANES)
    sub = lax.broadcasted_iota(jnp.int32, (SUB, LANES), 0)
    lane = lax.broadcasted_iota(jnp.int32, (SUB, LANES), 1)
    low = lane < LANES // 2
    edge_row = (0, ROWS - 1)

    def at_edge(offset, j, side, half):
        start = (SUB * half + offset) * STRIDE + j * ROWS + edge_row[side]
        return pl.ds(start, SUB, stride=STRIDE)

    def slots_of(half):
        return pl.ds(SUB * half, SUB)

    def chunk(d):
        return pl.ds(mine + CHUNK * lax.rem(xi + NX4 + d, NX4), CHUNK)

    def local(d):
        return CHUNK * lax.rem(xi + NX4 + d, NX4)


    def core_s():
        return remote("core_s", ps.at[pl.ds(theirs, HALF)], r1s, sibling)

    def core_pq():
        return remote("core_pq", pq.at[pl.ds(theirs, HALF)], r1pq, sibling)

    def core_e():
        return remote("core_e", pe.at[pl.ds(theirs, HALF)], r1e, sibling)

    def x_s(d):
        return remote(f"x_s{d}", ps.at[chunk(d)], r2s.at[d - 1], peer[d])

    def x_pq(d):
        return remote(f"x_pq{d}", pq.at[chunk(d)], r2pq.at[d - 1], peer[d])

    def x_e(d):
        return remote(f"x_e{d}", pe.at[chunk(d)], r2e.at[d - 1], peer[d])

    def z_swap(a, part, got):
        return remote(f"z_{a}", part, got, across)

    def gather(a, total, d, got=False):
        where = chunk(-d if got else 0)
        return remote(f"all_{a}{d}", total.at[where], total.at[where], peer[d])

    def forward(a, total, d, got=False):
        where = chunk(-d)
        if got:
            where = pl.ds(theirs + local(-d), CHUNK)
        return remote(f"fwd_{a}{d}", total.at[where], total.at[where], sibling)

    def halo(a, src, dst, side):
        return remote(f"halo_{a}{side}", src.at[side], dst.at[1 - side], toward[side])

    def add_chunk(total, got, d):
        for i in range(CHUNK):
            k = local(d) + i
            total[mine + k] = total[mine + k] + got[k]

    def first_pass(k, carry):
        j = lax.rem(theirs + k, BLKS)
        load(j).wait()
        acc = [jnp.zeros((PAIR, LANES), F32) for _ in range(TILES // 2)]
        for s in range(SLOTS):
            for r in range(TILES // 2):
                rows = pl.ds(PAIR * r, PAIR)
                c = e0[s + 1, j, rows, :] * act[s]
                e0[s + 1, j, rows, :] = c
                acc[r] = acc[r] + c * c
                x[s, j, rows, :LANES], x[s, j, rows, LANES:] = split(c)
        for r in range(TILES // 2):
            ps[j, pl.ds(PAIR * r, PAIR), :] = acc[r]
        for side in range(2):
            for half in range(2):
                h_eta[side, j, slots_of(half), :] = e0f[at_edge(1, j, side, half), :]
        return carry

    def planes(s, y):
        lhs = x[s].reshape(BLKS * ROWS, 2 * LANES)
        y[...] = jnp.dot(lhs, w[...], preferred_element_type=F32)

    def point(src, dst, dst_shift, s, y):
        gid = jnp.where(s < count, ids[s], -1)
        row = (s + 1) * STRIDE
        for j in range(BLKS):
            left = (j + BLKS - 1) % BLKS * ROWS
            right = (j + 1) % BLKS * ROWS
            for r in range(TILES):
                at = row + j * ROWS + SUB * r
                c = src[pl.ds(pl.multiple_of(at, SUB), SUB), :]
                up_x = src[pl.ds(at + 1, SUB), :]
                dn_x = src[pl.ds(at - 1, SUB), :]
                if r == TILES - 1:
                    up_x = jnp.where(sub == SUB - 1, 0.0, up_x)
                if r == 0:
                    dn_x = jnp.where(sub == 0, 0.0, dn_x)
                own = y[j * ROWS + SUB * r:j * ROWS + SUB * r + SUB, :LANES]
                spill = jnp.where(
                    low, y[left + SUB * r:left + SUB * r + SUB, LANES:],
                    y[right + SUB * r:right + SUB * r + SUB, LANES:])
                nb_sum = (up_x + dn_x) + (own + spill)
                labs = lab[pl.ds(SUB * r, SUB), j * LANES:j * LANES + LANES]
                mark = jnp.where(labs == gid, 0.15, 0.0).astype(F32)
                val = 0.15 * nb_sum + c * (0.175 + 0.15 * (c * c)) + mark
                dst[pl.ds(pl.multiple_of(at + dst_shift, SUB), SUB), :] = val

    def linear(src, dst, dst_shift, s_lo, s_hi):
        planes(s_lo, ya)

        def one(i, carry):
            s = s_lo + 2 * i
            planes(s + 1, yb)
            point(src, dst, dst_shift, s, ya)
            planes(jnp.minimum(s + 2, SLOTS - 1), ya)
            point(src, dst, dst_shift, s + 1, yb)
            return carry

        lax.fori_loop(0, lax.div(s_hi - s_lo, 2), one, 0)

    def sums_pass(j, carry):
        accp = [jnp.zeros((SUB, LANES), F32) for _ in range(TILES)]
        accq = [jnp.zeros((SUB, LANES), F32) for _ in range(TILES)]
        for s in range(SLOTS):
            for r in range(TILES):
                rows = pl.ds(SUB * r, SUB)
                u = e1[s + 1, j, rows, :]
                accp[r] = accp[r] + u * e0[s + 1, j, rows, :]
                accq[r] = accq[r] + u * u
        for r in range(TILES):
            pq[j, 0, pl.ds(SUB * r, SUB), :] = accp[r]
            pq[j, 1, pl.ds(SUB * r, SUB), :] = accq[r]
        return carry

    def edge_pass(j, carry):
        fix = jnp.zeros((SUB, LANES), F32)
        for side in range(2):
            dp = jnp.zeros((SUB, LANES), F32)
            dq = jnp.zeros((SUB, LANES), F32)
            for half in range(2):
                where = at_edge(1, j, side, half)
                add = 0.15 * g_eta[side, j, slots_of(half), :]
                old = e1f[where, :]
                new = old + add
                e1f[where, :] = new
                h_u[side, j, slots_of(half), :] = new
                dp = dp + add * h_eta[side, j, slots_of(half), :]
                dq = dq + add * (old + new)
            fix = jnp.where(sub == side, jnp.sum(dp, axis=0, keepdims=True), fix)
            fix = jnp.where(sub == side + 2, jnp.sum(dq, axis=0, keepdims=True), fix)
        pe[j] = fix
        return carry

    def second_pass(j, carry):
        tot = [0.225 * s1[j, pl.ds(PAIR * r, PAIR), :] for r in range(TILES // 2)]
        for s in range(SLOTS):
            for r in range(TILES // 2):
                rows = pl.ds(PAIR * r, PAIR)
                v = e1[s + 1, j, rows, :] - e0[s + 1, j, rows, :] * tot[r]
                e1[s + 1, j, rows, :] = v
                x[s, j, rows, :LANES], x[s, j, rows, LANES:] = split(v)
        return carry

    def last_edge_pass(j, carry):
        for side in range(2):
            tot = 0.225 * g_s[side, pl.ds(j, 1), :]
            for half in range(2):
                where = at_edge(0, j, side, half)
                out = g_u[side, j, slots_of(half), :] - g_eta[side, j, slots_of(half), :] * tot
                u2f[where, :] = u2f[where, :] + 0.15 * out
        return carry

    lax.fori_loop(0, BLKS, first_pass, 0)
    ids_copy.wait()
    lab_copy.wait()
    linear(e0f, e1f, 0, 0, 2)
    pl.semaphore_wait(barrier, len(partners))
    core_s().start()
    for side in range(2):
        halo("eta", h_eta, g_eta, side).start()
    linear(e0f, e1f, 0, 2, 6)

    core_s().wait_recv()
    for d in (2, 1, 3):
        add_chunk(ps, r1s, d)
        x_s(d).start()
    add_chunk(ps, r1s, 0)
    linear(e0f, e1f, 0, 6, SLOTS)

    lax.fori_loop(theirs, theirs + HALF, sums_pass, 0)
    core_pq().start()
    lax.fori_loop(mine, mine + HALF, sums_pass, 0)

    for d in (1, 3, 2):
        x_s(d).wait_recv()
    for i in range(CHUNK):
        k = mine + local(0) + i
        part_s[i] = (ps[k] + r2s[1, i]) + (r2s[0, i] + r2s[2, i])
    z_swap("s", part_s, z_s).start()

    core_pq().wait_recv()
    for d in (2, 1, 3):
        add_chunk(pq, r1pq, d)
        x_pq(d).start()
    add_chunk(pq, r1pq, 0)

    for side in range(2):
        halo("eta", h_eta, g_eta, side).wait_recv()
    lax.fori_loop(0, HALF, lambda k, c: edge_pass(theirs + k, c), 0, unroll=True)
    core_e().start()
    lax.fori_loop(0, HALF, lambda k, c: edge_pass(mine + k, c), 0, unroll=True)
    for side in range(2):
        halo("u", h_u, g_u, side).start()
    core_e().wait_recv()
    for d in (2, 1, 3):
        add_chunk(pe, r1e, d)
        x_e(d).start()
    add_chunk(pe, r1e, 0)

    z_swap("s", part_s, z_s).wait_recv()
    for i in range(CHUNK):
        s1[mine + local(0) + i] = part_s[i] + z_s[i]
    for d in (2, 1, 3):
        gather("s", s1, d).start()
    forward("s", s1, 0).start()

    for d in (1, 3, 2):
        x_pq(d).wait_recv()
    for d in (1, 3, 2):
        x_e(d).wait_recv()
    for i in range(CHUNK):
        k = mine + local(0) + i
        s = 0.45 * s1[k]
        p_sum = (pq[k, 0] + r2pq[1, i, 0]) + (r2pq[0, i, 0] + r2pq[2, i, 0])
        q_sum = (pq[k, 1] + r2pq[1, i, 1]) + (r2pq[0, i, 1] + r2pq[2, i, 1])
        part_t[i] = q_sum - s * p_sum
        fix = (pe[k] + r2e[1, i]) + (r2e[0, i] + r2e[2, i])
        for side, row in enumerate(edge_row):
            part_t[i, row:row + 1, :] = part_t[i, row:row + 1, :] + (
                fix[side + 2:side + 3] - 0.45 * s1[k, row:row + 1, :] * fix[side:side + 1])
    z_swap("t", part_t, z_t).start()

    for d in (1, 3, 2):
        gather("s", s1, d, True).wait_recv()
        forward("s", s1, d).start()
    lax.fori_loop(mine, mine + HALF, second_pass, 0)

    z_swap("t", part_t, z_t).wait_recv()
    for i in range(CHUNK):
        k = mine + local(0) + i
        s = s1[k]
        s2[k] = (part_t[i] + z_t[i]) + 0.050625 * (s * s * s)
    for d in (2, 1, 3):
        gather("t", s2, d).start()
    forward("t", s2, 0).start()

    for d in range(4):
        forward("s", s1, d, True).wait_recv()
    for side, row in enumerate(edge_row):
        for j in range(BLKS):
            h_s[side, j:j + 1, :] = s1[j, row:row + 1, :]
        halo("s", h_s, g_s, side).start()
    lax.fori_loop(theirs, theirs + HALF, second_pass, 0)
    linear(e1f, u2f, -STRIDE, 0, 12)

    for d in (1, 3, 2):
        gather("t", s2, d, True).wait_recv()
        forward("t", s2, d).start()
    linear(e1f, u2f, -STRIDE, 12, SLOTS)
    for side in range(2):
        halo("u", h_u, g_u, side).wait_recv()
        halo("s", h_s, g_s, side).wait_recv()
    lax.fori_loop(0, BLKS, last_edge_pass, 0, unroll=8)
    for d in range(4):
        forward("t", s2, d, True).wait_recv()

    core_s().wait_send()
    core_pq().wait_send()
    core_e().wait_send()
    for d in (1, 2, 3):
        x_s(d).wait_send()
        x_pq(d).wait_send()
        x_e(d).wait_send()
        gather("s", s1, d).wait_send()
        gather("t", s2, d).wait_send()
    z_swap("s", part_s, z_s).wait_send()
    z_swap("t", part_t, z_t).wait_send()
    for d in range(4):
        forward("s", s1, d).wait_send()
        forward("t", s2, d).wait_send()
    for side in range(2):
        halo("eta", h_eta, g_eta, side).wait_send()
        halo("u", h_u, g_u, side).wait_send()
        halo("s", h_s, g_s, side).wait_send()


def last(e1, u2, s2, out, stage, sem):
    def copy(s):
        return pltpu.make_async_copy(stage.at[s], out.at[s], sem.at[s])

    def one(s, carry):
        def blocks(j, carry):
            cols = pl.ds(pl.multiple_of(j * LANES, LANES), LANES)
            for r in range(TILES):
                rows = pl.ds(SUB * r, SUB)
                stage[s, rows, cols] = u2[s, j, rows, :] - e1[s + 1, j, rows, :] * (0.225 * s2[j, rows, :])
            return carry
        lax.fori_loop(0, BLKS, blocks, 0, unroll=4)
        copy(s).start()
        return carry

    lax.fori_loop(0, SLOTS, one, 0)

    def drain(s, carry):
        copy(s).wait()
        return carry
    lax.fori_loop(0, SLOTS, drain, 0)


def body(order, grain_ids, counts, labels):
    hbm = pl.BlockSpec(memory_space=pltpu.HBM)
    smem = pl.BlockSpec(memory_space=pltpu.SMEM)
    vmem = pl.BlockSpec(memory_space=pltpu.VMEM)
    grain_ids = pltpu.with_memory_space_constraint(grain_ids, pltpu.HBM)
    order = pltpu.with_memory_space_constraint(order, pltpu.HBM)
    labels = pltpu.with_memory_space_constraint(labels, pltpu.HBM)

    def f32(*shape):
        return pltpu.VMEM(shape, F32)

    e1, u2, s2 = pl.pallas_call(
        kernel,
        out_shape=(
            f32(SLOTS + 2, BLKS, ROWS, LANES),
            f32(SLOTS + 1, BLKS, ROWS, LANES),
            f32(BLKS, ROWS, LANES),
        ),
        in_specs=[hbm, hbm, smem, hbm],
        out_specs=(vmem, vmem, vmem),
        scratch_shapes=[
            pltpu.SMEM((SLOTS,), jnp.int32),
            pltpu.VMEM((2 * LANES, 2 * LANES), BF16),
            pltpu.VMEM((SLOTS, BLKS, ROWS, 2 * LANES), BF16),
            f32(BLKS * ROWS, 2 * LANES),
            f32(BLKS * ROWS, 2 * LANES),
            f32(SLOTS + 2, BLKS, ROWS, LANES),
            pltpu.VMEM((ROWS, BLKS * LANES), jnp.int32),
            f32(BLKS, ROWS, LANES),
            f32(BLKS, 2, ROWS, LANES),
            f32(BLKS, SUB, LANES),
            f32(HALF, ROWS, LANES),
            f32(HALF, 2, ROWS, LANES),
            f32(HALF, SUB, LANES),
            f32(3, CHUNK, ROWS, LANES),
            f32(3, CHUNK, 2, ROWS, LANES),
            f32(3, CHUNK, SUB, LANES),
            f32(CHUNK, ROWS, LANES),
            f32(CHUNK, ROWS, LANES),
            f32(CHUNK, ROWS, LANES),
            f32(CHUNK, ROWS, LANES),
            f32(BLKS, ROWS, LANES),
            f32(2, BLKS, SLOTS, LANES),
            f32(2, BLKS, SLOTS, LANES),
            f32(2, BLKS, SLOTS, LANES),
            f32(2, BLKS, SLOTS, LANES),
            f32(2, BLKS, LANES),
            f32(2, BLKS, LANES),
            pltpu.SemaphoreType.DMA((BLKS,)),
            pltpu.SemaphoreType.DMA,
            pltpu.SemaphoreType.DMA,
            pltpu.SemaphoreType.DMA((len(NAMES),)),
            pltpu.SemaphoreType.DMA((len(NAMES),)),
        ],
        compiler_params=pltpu.CompilerParams(
            collective_id=0, has_side_effects=True, vmem_limit_bytes=40 * 1024 * 1024),
        name="steps",
    )(order, grain_ids, counts, labels)
    return pl.pallas_call(
        last,
        out_shape=jax.ShapeDtypeStruct(order.shape, F32),
        in_specs=[vmem, vmem, vmem],
        out_specs=hbm,
        scratch_shapes=[
            pltpu.VMEM((SLOTS, ROWS, BLKS * LANES), F32),
            pltpu.SemaphoreType.DMA((SLOTS,)),
        ],
        compiler_params=pltpu.CompilerParams(vmem_limit_bytes=32 * 1024 * 1024),
        name="last",
    )(e1, u2, s2)


def solution(mesh):
    placed = (P("grain", "blk", None), P("grain"), P("grain"), P("blk", None))
    return jax.shard_map(
        body, mesh=mesh, in_specs=placed, out_specs=P("grain", "blk", None), check_vma=False
    )
```
